32 devices in a mesh: blk: 4 (over y, x), leaf: 8 (over z, core).
Axes of the slice: x: 2, y: 2, z: 4, core: 2. Of those that a mesh axis runs over, the one named last changes fastest.
Arguments:
- points: bfloat16 [3, 16384], P(None, ('blk', 'leaf')), may hold values from 0 to 1
- test_matrix: bfloat16 [16384, 512], P(('blk', 'leaf')), may hold values from -6 to 6
- near_lists: int32 [64, 5], P(('blk', 'leaf')), may hold values from 0 to 5, as said below
- leaf_pivots: int32 [32, 256], P(('blk', 'leaf')), may hold values from 0 to 511, as said below
- leaf_proj: bfloat16 [16384, 256], P(('blk', 'leaf')), may hold values from -0.25 to 0.25
- merge_pivots: int32 [3, 32, 256], P(None, ('blk', 'leaf')), may hold values from 0 to 511, as said below
- merge_proj: bfloat16 [3, 32, 512, 256], P(None, ('blk', 'leaf')), as said below
Outputs:
- sample: bfloat16 [16384, 512], P(('blk', 'leaf'))
- top_samples: float32 [8192, 512], P(('blk', 'leaf'))
- top_omega: float32 [8192, 512], P(('blk', 'leaf'))
The draws below stay inside these ranges and needn't reach their ends.
Inputs may be any that keep to these rules, and one draw needn't show every extreme that they name: `near_lists`: the 5 entries of one row are distinct. `leaf_pivots`: the 256 entries of one row are distinct. `merge_pivots`: the 256 entries of one row are distinct; rows [t, n] are equal for all n with the same n // 2^(t+1). `merge_proj`: matrices [t, n] are equal for all n with the same n // 2^(t+1); entries lie within -4 / sqrt(512) to 4 / sqrt(512).
All inputs are finite; a program needn't handle non-finite values.
Results may differ from the reference program's by a relative error of at most 0.0048.
Values may be sent and summed in bfloat16 or wider, within the bound.
No kernel may reach another device: no remote copies, remote signals or barrier semaphores. Data moves between devices by JAX's collectives and lax.ppermute only.
A program may use at most 64 MiB of HBM per device.

```python
import math
import jax
import jax.numpy as jnp
from jax import lax

BS = 256
RBD = 2
R = 512
K = 256
NNB = 5
LEVELS = 3
NODES = 32
NBLOCKS = 64
NPTS = 16384
N_BLK = 4
N_LEAF = 8


def draw_near_lists(key, part):
    key_list = jax.random.split(key, NBLOCKS)
    chosen = jax.vmap(lambda sub_key: jax.random.permutation(sub_key, 3 * RBD))(key_list)
    return chosen[:, :NNB].astype(jnp.int32)


def draw_leaf_pivots(key, part):
    key_list = jax.random.split(key, NODES)
    chosen = jax.vmap(lambda sub_key: jax.random.permutation(sub_key, RBD * BS))(key_list)
    return chosen[:, :K].astype(jnp.int32)


def node_keys(key, tree_level, salt_value):
    base_key = jax.random.fold_in(key, salt_value + tree_level)
    groups = jnp.arange(NODES, dtype=jnp.int32) // 2 ** (tree_level + 1)
    return jax.vmap(lambda group_id: jax.random.fold_in(base_key, group_id))(groups)


def draw_merge_pivots(key, part):
    stacked_levels = []
    for tree_level in range(LEVELS):
        key_list = node_keys(key, tree_level, 11)
        chosen = jax.vmap(lambda sub_key: jax.random.permutation(sub_key, 2 * K))(key_list)
        stacked_levels.append(chosen[:, :K])
    return jnp.stack(stacked_levels).astype(jnp.int32)


def draw_merge_proj(key, part):
    spread_factor = (2.0 * K) ** (-0.5)
    stacked_levels = []
    for tree_level in range(LEVELS):
        key_list = node_keys(key, tree_level, 71)
        values_drawn = jax.vmap(lambda sub_key: jnp.clip(jax.random.normal(sub_key, (2 * K, K), jnp.float32), -3.9, 3.9))(key_list)
        stacked_levels.append(values_drawn * spread_factor)
    return jnp.stack(stacked_levels).astype(jnp.bfloat16)


def block_levels(stream_key, shape, shards, low, high):
    def one(axis_at, blocks):
        draws = jax.random.uniform(jax.random.fold_in(jax.random.fold_in(stream_key, 6), axis_at), (blocks,), jnp.float32, low / len(shards), high / len(shards))
        return jnp.repeat(jnp.exp(draws), shape[axis_at] // blocks).reshape((-1,) + (1,) * (len(shape) - axis_at - 1))

    gain = one(*shards[0])
    for cut in shards[1:]:
        gain = gain * one(*cut)
    return gain


def normal_values(own_key, extent, scale, limit, pieces=(), kind=jnp.bfloat16):
    result = jax.random.normal(own_key, extent, jnp.float32) * scale
    if len(pieces) > 0:
        result = block_levels(own_key, extent, pieces, -0.22, 0.18) * result
    return jnp.clip(result, min=-limit, max=limit).astype(kind)


def setup_inputs(seed: int = 0) -> dict:
    seeds = jax.random.split(jax.random.key(seed), 8)
    return {
        "points": jnp.clip(1.0 * jax.random.uniform(seeds[0], (3, NPTS), jnp.float32) ** block_levels(seeds[0], (3, NPTS), ((1, 32),), -0.2, 0.2), 0.0, 1.0).astype(jnp.bfloat16),
        "test_matrix": normal_values(seeds[1], (NPTS, R), 1.0, 6.0, ((0, 32),)),
        "near_lists": draw_near_lists(jax.random.fold_in(seeds[7], 71), 0),
        "leaf_pivots": draw_leaf_pivots(jax.random.fold_in(seeds[7], 71), 0),
        "leaf_proj": normal_values(seeds[4], (NPTS, K), (RBD * BS) ** -0.5, 0.25, ((0, 32),)),
        "merge_pivots": draw_merge_pivots(jax.random.fold_in(seeds[7], 71), 0),
        "merge_proj": draw_merge_proj(jax.random.fold_in(seeds[7], 71), 0),
    }


SPREAD = 25.0

def kernel_block(row_points, col_points):
    offsets = row_points[..., :, :, None] - col_points[..., :, None, :]
    return jnp.exp(-SPREAD * lax.optimization_barrier(jnp.sum(offsets * offsets, axis=-3)))

def select_rows(matrix_in, index_in):
    return matrix_in[index_in]

def select_columns(matrix_in, index_in):
    return matrix_in[:, index_in]

def reference(points, test_matrix, near_lists, leaf_pivots, leaf_proj, merge_pivots, merge_proj):
    near_amp = 9.0 / math.sqrt(NNB * BS)
    far_amp = 3.0 / math.sqrt(K)
    row_count = RBD * BS
    points_grid = points.astype(jnp.float32).reshape(3, N_BLK, N_LEAF, RBD, BS)
    matrix_grid = test_matrix.reshape(N_BLK, N_LEAF, RBD, BS, R)
    lists_grid = near_lists.reshape(N_BLK, N_LEAF, RBD, NNB)
    pivots_grid = leaf_pivots.reshape(N_BLK, N_LEAF, K)
    proj_grid = leaf_proj.reshape(N_BLK, N_LEAF, row_count, K)

    def one_device(device_index):
        blk_index = device_index // N_LEAF
        leaf_index = device_index % N_LEAF
        sources = [(blk_index + N_BLK - 1) % N_BLK, blk_index, (blk_index + 1) % N_BLK]
        wide_matrix = jnp.concatenate([matrix_grid[source, leaf_index] for source in sources], axis=0)
        wide_points = jnp.concatenate([jnp.transpose(points_grid[:, source, leaf_index], (1, 0, 2)) for source in sources], axis=0)
        own_points = jnp.transpose(points_grid[:, blk_index, leaf_index], (1, 0, 2))
        lists_here = lists_grid[blk_index, leaf_index]
        full_sum = jnp.zeros((RBD, BS, R), jnp.float32)
        remote_sum = jnp.zeros((RBD, BS, R), jnp.float32)
        for entry_slot in range(NNB):
            candidate = lists_here[:, entry_slot]
            near_block = (near_amp * kernel_block(own_points, wide_points[candidate])).astype(jnp.bfloat16)
            term_block = jnp.einsum('ipq,iqr->ipr', near_block.astype(jnp.float32), wide_matrix[candidate].astype(jnp.float32))
            is_remote = (candidate // RBD != 1).astype(jnp.float32)[:, None, None]
            full_sum = full_sum + term_block
            remote_sum = remote_sum + is_remote * term_block
        remote_rows = remote_sum.reshape(row_count, R)
        pivots = pivots_grid[blk_index, leaf_index]
        samples = remote_rows[pivots]
        skeleton = points_grid[:, blk_index, leaf_index].reshape(3, row_count)[:, pivots]
        compressed = jnp.dot(proj_grid[blk_index, leaf_index].T, matrix_grid[blk_index, leaf_index].reshape(row_count, R), preferred_element_type=jnp.float32)
        return (full_sum.reshape(row_count, R).astype(jnp.bfloat16), samples, compressed, skeleton)
    sample, samples, compressed, skeleton = lax.map(one_device, jnp.arange(NODES, dtype=jnp.int32))
    samples = samples.reshape(N_BLK, N_LEAF, K, R)
    compressed = compressed.reshape(N_BLK, N_LEAF, K, R)
    skeleton = skeleton.reshape(N_BLK, N_LEAF, 3, K)
    pivots_all = merge_pivots.reshape(LEVELS, N_BLK, N_LEAF, K)
    proj_all = merge_proj.reshape(LEVELS, N_BLK, N_LEAF, 2 * K, K)
    highest = lax.Precision.HIGHEST
    for tree_level in range(1, LEVELS + 1):
        group_count = N_LEAF >> tree_level
        paired = samples.reshape(N_BLK, group_count, 2, K, R)
        paired_comp = compressed.reshape(N_BLK, group_count, 2, K, R)
        paired_skel = skeleton.reshape(N_BLK, group_count, 2, 3, K)
        coupling = far_amp * kernel_block(paired_skel[:, :, 0], paired_skel[:, :, 1])
        upper_half = paired[:, :, 0] - jnp.einsum('bnpq,bnqr->bnpr', coupling, paired_comp[:, :, 1], precision=highest)
        lower_half = paired[:, :, 1] - jnp.einsum('bnqp,bnqr->bnpr', coupling, paired_comp[:, :, 0], precision=highest)
        stacked = jnp.concatenate([upper_half, lower_half], axis=2)
        pivots = pivots_all[tree_level - 1].reshape(N_BLK, group_count, 2 ** tree_level, K)[:, :, 0]
        projection = proj_all[tree_level - 1].reshape(N_BLK, group_count, 2 ** tree_level, 2 * K, K)[:, :, 0].astype(jnp.float32)
        samples = jax.vmap(jax.vmap(select_rows))(stacked, pivots)
        joined = jnp.concatenate([paired_skel[:, :, 0], paired_skel[:, :, 1]], axis=3)
        skeleton = jax.vmap(jax.vmap(select_columns))(joined, pivots)
        compressed = jnp.einsum('bnqp,bnqr->bnpr', projection, paired_comp.reshape(N_BLK, group_count, 2 * K, R), precision=highest)
    repeats = 2 ** LEVELS
    top_samples = jnp.repeat(samples, repeats, axis=1).reshape(NODES * K, R)
    top_omega = jnp.repeat(compressed, repeats, axis=1).reshape(NODES * K, R)
    return (sample.reshape(NPTS, R), top_samples, top_omega)
```

```python
import functools
import math

import jax
import jax.numpy as jnp
from jax import lax
from jax.experimental import pallas as pl
from jax.experimental.pallas import tpu as pltpu
from jax.sharding import PartitionSpec as P

SPREAD = 25.0
EXPONENT = -SPREAD * math.log2(math.e)
FAR_OFF = 1024.0
HEIGHT = 16
ROW_HI, ROW_LO, MEET, PIVOT = 3, 4, 5, 6
BF16, F32 = jnp.bfloat16, jnp.float32


def call(body, outs, flops, *args):
    specs = [
        pl.BlockSpec(memory_space=pltpu.SMEM if a.dtype == jnp.int32 and a.ndim == 2 and a.shape[1] < 128 else pltpu.VMEM)
        for a in args
    ]
    moved = sum(a.size * a.dtype.itemsize for a in args) + sum(
        math.prod(s) * jnp.dtype(d).itemsize for s, d in outs
    )
    return pl.pallas_call(
        body,
        out_shape=[jax.ShapeDtypeStruct(s, d) for s, d in outs],
        in_specs=specs,
        out_specs=[pl.BlockSpec(memory_space=pltpu.VMEM)] * len(outs),
        compiler_params=pltpu.CompilerParams(vmem_limit_bytes=40 << 20),
        cost_estimate=pl.CostEstimate(flops=flops, bytes_accessed=moved, transcendentals=0),
    )(*args)


def dot(a, b, over_a=1, over_b=0):
    return lax.dot_general(a, b, (((over_a,), (over_b,)), ((), ())), preferred_element_type=F32)


def halves(x):
    hi = x.astype(BF16)
    return hi, (x - hi.astype(F32)).astype(BF16)


def rows_of(entries, width):
    row = lax.broadcasted_iota(jnp.int32, (HEIGHT, width), 0)
    out = jnp.zeros((HEIGHT, width), F32)
    for k, entry in enumerate(entries):
        out = jnp.where(row == k, entry, out)
    return out


def norm_parts(p):
    n = p[0:1] * p[0:1] + p[1:2] * p[1:2] + p[2:3] * p[2:3]
    hi = n.astype(BF16).astype(F32)
    mid = (n - hi).astype(BF16).astype(F32)
    return [hi, mid, n - hi - mid]


def left_features(p, penalties):
    entries = [p[0:1], p[1:2], p[2:3], *norm_parts(p), 1.0, 1.0, 1.0, *penalties]
    return rows_of(entries, p.shape[1]).astype(BF16)


def right_features(p, marks):
    entries = [-2.0 * p[0:1], -2.0 * p[1:2], -2.0 * p[2:3], 1.0, 1.0, 1.0, *norm_parts(p), *marks]
    return rows_of(entries, p.shape[1]).astype(BF16)


def gauss(left, right, amp):
    return jnp.exp2(EXPONENT * dot(left, right, 0, 0)) * amp


def lane_index(width):
    return lax.broadcasted_iota(jnp.int32, (1, width), 1)


def chosen(attributes, index):
    spot = lax.broadcasted_iota(jnp.int32, (attributes.shape[1], index.shape[1]), 0)
    one_hot = jnp.where(spot == index, 1.0, 0.0).astype(BF16)
    return dot(attributes.astype(BF16), one_hot)


def bit_of(value, place):
    return (value >> place) & 1


def describe_body(points_ref, pivots_ref, merges_ref, out_ref):
    p = points_ref[...].astype(F32)
    width = p.shape[1]
    rank = pivots_ref.shape[1]
    spot = lane_index(width)
    attributes = rows_of(
        [p[0:1], p[1:2], p[2:3], (spot // rank).astype(F32), (spot % rank).astype(F32)], width
    )
    skeleton = chosen(attributes, pivots_ref[...])
    row = lax.broadcasted_iota(jnp.int32, skeleton.shape, 0)
    for level in range(merges_ref.shape[0] - 1):
        q = merges_ref[level]
        skeleton = jnp.where(row == PIVOT + 2 * level, (q // rank).astype(F32), skeleton)
        skeleton = jnp.where(row == PIVOT + 2 * level + 1, (q % rank).astype(F32), skeleton)
    out_ref[...] = skeleton.astype(BF16)


def compress_body(proj_ref, matrix_ref, merge_ref, *outs):
    position = lax.axis_index("leaf")
    levels = merge_ref.shape[0]
    rank = proj_ref.shape[1]
    c = dot(proj_ref[...], matrix_ref[...], 0, 0)
    for level in range(levels):
        hi, lo = halves(c)
        outs[0][pl.ds(level * rank, rank), :] = hi
        outs[1][pl.ds(level * rank, rank), :] = lo
        start = pl.multiple_of(bit_of(position, level) * rank, rank)
        m = merge_ref[level, 0, pl.ds(start, rank), :]
        c = dot(m, hi, 0, 0) + dot(m, lo, 0, 0)
    outs[2][...] = c


def tree_body(far_amp, md_ref, merges_ref, hi_ref, lo_ref, top_ref, part_ref):
    position = lax.axis_index("leaf")
    levels = merges_ref.shape[0]
    rank = merges_ref.shape[2]
    nodes = [md_ref[k].astype(F32) for k in range(md_ref.shape[0])]
    pivots = nodes
    row = lax.broadcasted_iota(jnp.int32, (HEIGHT, rank), 0)
    path = []
    for level in range(levels):
        path.append(nodes[0])
        flip = bit_of(position, level)
        merged = []
        for j in range(len(nodes) // 2):
            if level < levels - 1:
                source = pivots[j << level + 1]
                k = PIVOT + 2 * level
                q = (source[k : k + 1] * rank + source[k + 1 : k + 2]).astype(jnp.int32)
            else:
                q = merges_ref[level]
            q = jnp.where(flip == 1, jnp.where(q < rank, q + rank, q - rank), q)
            far = jnp.where(row == MEET, float(level + 1), nodes[2 * j + 1])
            merged.append(chosen(jnp.concatenate([nodes[2 * j], far], axis=1), q))
        nodes = merged
    top = nodes[0]
    top_ref[...] = top
    total = jnp.zeros(part_ref.shape, F32)
    for level in range(levels):
        penalty = jnp.where(top[MEET : MEET + 1] == float(level + 1), 0.0, FAR_OFF)
        block = gauss(left_features(top, [penalty]), right_features(path[level], [1.0]), -far_amp)
        block_hi, block_lo = halves(block)
        hi = hi_ref[pl.ds(level * rank, rank), :]
        lo = lo_ref[pl.ds(level * rank, rank), :]
        total += dot(block_hi, hi) + dot(block_hi, lo) + dot(block_lo, hi)
    part_ref[...] = total


def penalty_table(lists_ref, base, blocks):
    table = []
    for i in range(blocks):
        line = []
        for k in range(blocks):
            listed = lists_ref[i, 0] == base + k
            for slot in range(1, lists_ref.shape[1]):
                listed |= lists_ref[i, slot] == base + k
            line.append(jnp.where(listed, 0.0, FAR_OFF))
        table.append(line)
    return table


def per_block(block_index, values):
    out = jnp.zeros(block_index.shape, F32)
    for i, value in enumerate(values):
        out = jnp.where(block_index == i, value, out)
    return out


def near_body(near_amp, even_ahead, lists_ref, own_ref, first_ref, second_ref, top_ref, matrix_ref, *outs):
    near_first, near_second, top_first, top_second, own_terms = outs
    blocks = lists_ref.shape[0]
    own = own_ref[...].astype(F32)
    width = own.shape[1]
    block_rows = width // blocks
    spot = lane_index(width) // block_rows
    marks = [jnp.where(spot == k, 1.0, 0.0) for k in range(blocks)]
    top = top_ref[...]
    top_block = top[ROW_HI : ROW_HI + 1].astype(jnp.int32)
    top_here = top[MEET : MEET + 1] == 0.0
    if even_ahead:
        odd = lax.axis_index("blk") % 2
        bases = [2 * blocks * (1 - odd), 2 * blocks * odd]
    else:
        bases = [0, 2 * blocks]
    for ref, base, near_ref, part_ref in (
        (first_ref, bases[0], near_first, top_first),
        (second_ref, bases[1], near_second, top_second),
    ):
        table = penalty_table(lists_ref, base, blocks)
        columns = right_features(ref[0:3, :].astype(F32), marks)
        penalties = [per_block(spot, [table[i][k] for i in range(blocks)]) for k in range(blocks)]
        near_ref[...] = gauss(left_features(own, penalties), columns, near_amp).astype(BF16)
        penalties = [
            jnp.where(top_here, per_block(top_block, [table[i][k] for i in range(blocks)]), FAR_OFF)
            for k in range(blocks)
        ]
        part_ref[...] = gauss(left_features(top, penalties), columns, near_amp).astype(BF16)
    table = penalty_table(lists_ref, blocks, blocks)
    penalties = [per_block(spot, [table[i][k] for i in range(blocks)]) for k in range(blocks)]
    near_own = gauss(left_features(own, penalties), right_features(own, marks), near_amp).astype(BF16)
    own_terms[...] = dot(near_own, matrix_ref[...])


def product_body(skip, *refs):
    start_ref, first_ref, second_ref, *chunks, out_ref = refs
    total = start_ref[...]
    per_side = len(chunks) // 2
    for side, left_ref in enumerate((first_ref, second_ref)):
        at = 0
        for k, chunk_ref in enumerate(chunks[side * per_side : (side + 1) * per_side]):
            lead = skip if k == 0 else 0
            count = chunk_ref.shape[0] - lead
            total += dot(left_ref[:, at : at + count], chunk_ref[lead:, :])
            at += count
    out_ref[...] = total.astype(out_ref.dtype)


def permuted(block, axis, route):
    return lax.ppermute(block, axis, [(route(i), i) for i in range(lax.axis_size(axis))])


def swapped(block, distance):
    return permuted(block, "leaf", lambda i: i ^ distance)


def group_sum(part, levels):
    second = bit_of(lax.axis_index("leaf"), 0) == 1
    middle = part.shape[1] // 2
    low, high = part[:, :middle], part[:, middle:]
    kept = jnp.where(second, high, low)
    given = jnp.where(second, low, high).astype(BF16)
    mine = (kept + swapped(given, 1).astype(F32)).astype(BF16)
    total = mine.astype(F32)
    for distance in range(2, 1 << levels, 2):
        total = total + swapped(mine, distance).astype(F32)
    other = swapped(total.astype(BF16), 1).astype(F32)
    return jnp.where(
        second, jnp.concatenate([other, total], axis=1), jnp.concatenate([total, other], axis=1)
    )


def on_device(points, test_matrix, near_lists, leaf_pivots, leaf_proj, merge_pivots, merge_proj):
    row_count, sample_count = test_matrix.shape
    block_count, slot_count = near_lists.shape
    skel_rank = leaf_pivots.shape[1]
    level_count = merge_pivots.shape[0]
    near_amp = 9.0 / math.sqrt(slot_count * (row_count // block_count))
    far_amp = 3.0 / math.sqrt(skel_rank)
    square = 2 * skel_rank * skel_rank * sample_count

    count = lax.axis_size("blk")
    paired = count % 2 == 0 and count > 2
    lead = HEIGHT
    headed = jnp.concatenate([jnp.pad(points, ((0, lead - 3), (0, 0))), test_matrix], axis=0)
    if paired:
        cut = row_count // 4
        edges = [0, lead + cut, lead + 2 * cut, lead + 3 * cut, lead + 4 * cut]
        chunks = [headed[a:b] for a, b in zip(edges[:-1], edges[1:])]
        step = lambda i, by: (i + (by if i % 2 == 0 else -by)) % count
        first = [permuted(c, "blk", lambda i: step(i, 1)) for c in chunks[:3]]
        straight = permuted(chunks[3], "blk", lambda i: step(i, -1))
        first.append(permuted(chunks[3], "blk", lambda i: step(i, 1)))
        second = [permuted(c, "blk", lambda i: step(i, -2)) for c in first[:3]]
        second.append(straight)
    else:
        first = [permuted(headed, "blk", lambda i: (i - 1) % count)]
        second = [permuted(headed, "blk", lambda i: (i + 1) % count)]

    (own_md,) = call(
        describe_body, [((HEIGHT, skel_rank), BF16)], 0, points, leaf_pivots, merge_pivots
    )
    pair = jnp.stack([own_md, swapped(own_md, 1)])
    md = jnp.concatenate([pair] + [swapped(pair, d) for d in range(2, 1 << level_count, 2)], axis=0)

    hi, lo, omega_part = call(
        compress_body,
        [((level_count * skel_rank, sample_count), BF16)] * 2 + [((skel_rank, sample_count), F32)],
        8 * square,
        leaf_proj,
        test_matrix,
        merge_proj,
    )
    top_omega = group_sum(omega_part, level_count)
    top, far_part = call(
        functools.partial(tree_body, far_amp),
        [((HEIGHT, skel_rank), F32), ((skel_rank, sample_count), F32)],
        9 * square,
        md,
        merge_pivots,
        hi,
        lo,
    )
    near_first, near_second, top_first, top_second, own_terms = call(
        functools.partial(near_body, near_amp, paired),
        [((row_count, row_count), BF16)] * 2
        + [((skel_rank, row_count), BF16)] * 2
        + [((row_count, sample_count), F32)],
        8 * square,
        near_lists,
        points,
        first[0],
        second[0],
        top,
        test_matrix,
    )
    product = functools.partial(product_body, lead)
    (samples_part,) = call(
        product, [((skel_rank, sample_count), F32)], 4 * square, far_part, top_first, top_second, *first, *second
    )
    top_samples = group_sum(samples_part, level_count)
    (sample,) = call(
        product, [((row_count, sample_count), BF16)], 8 * square, own_terms, near_first, near_second, *first, *second
    )
    return (sample, top_samples, top_omega)


def solution(mesh):
    placed = (
        P(None, ("blk", "leaf")),
        P(("blk", "leaf"), None),
        P(("blk", "leaf"), None),
        P(("blk", "leaf"), None),
        P(("blk", "leaf"), None),
        P(None, ("blk", "leaf"), None),
        P(None, ("blk", "leaf"), None, None),
    )
    return jax.shard_map(
        on_device,
        mesh=mesh,
        in_specs=placed,
        out_specs=(P(("blk", "leaf"), None), P(("blk", "leaf"), None), P(("blk", "leaf"), None)),
        check_vma=False,
    )
```

```python
import functools
import math

import jax
import jax.numpy as jnp
from jax import lax
from jax.experimental import pallas as pl
from jax.experimental.pallas import tpu as pltpu
from jax.sharding import PartitionSpec as P

SPREAD = 25.0
EXPONENT = -SPREAD * math.log2(math.e)
FAR_OFF = 1024.0
HEIGHT = 16
ROW_HI, ROW_LO, MEET, PIVOT = 3, 4, 5, 6
BF16, F32 = jnp.bfloat16, jnp.float32


def call(body, outs, flops, *args):
    specs = [
        pl.BlockSpec(memory_space=pltpu.SMEM if a.dtype == jnp.int32 and a.ndim == 2 and a.shape[1] < 128 else pltpu.VMEM)
        for a in args
    ]
    moved = sum(a.size * a.dtype.itemsize for a in args) + sum(
        math.prod(s) * jnp.dtype(d).itemsize for s, d in outs
    )
    return pl.pallas_call(
        body,
        out_shape=[jax.ShapeDtypeStruct(s, d) for s, d in outs],
        in_specs=specs,
        out_specs=[pl.BlockSpec(memory_space=pltpu.VMEM)] * len(outs),
        compiler_params=pltpu.CompilerParams(vmem_limit_bytes=40 << 20),
        cost_estimate=pl.CostEstimate(flops=flops, bytes_accessed=moved, transcendentals=0),
    )(*args)


def dot(a, b, over_a=1, over_b=0):
    return lax.dot_general(a, b, (((over_a,), (over_b,)), ((), ())), preferred_element_type=F32)


def halves(x):
    hi = x.astype(BF16)
    return hi, (x - hi.astype(F32)).astype(BF16)


def rows_of(entries, width):
    row = lax.broadcasted_iota(jnp.int32, (HEIGHT, width), 0)
    out = jnp.zeros((HEIGHT, width), F32)
    for k, entry in enumerate(entries):
        out = jnp.where(row == k, entry, out)
    return out


def norm_parts(p):
    n = p[0:1] * p[0:1] + p[1:2] * p[1:2] + p[2:3] * p[2:3]
    hi = n.astype(BF16).astype(F32)
    mid = (n - hi).astype(BF16).astype(F32)
    return [hi, mid, n - hi - mid]


def left_features(p, penalties):
    entries = [p[0:1], p[1:2], p[2:3], *norm_parts(p), 1.0, 1.0, 1.0, *penalties]
    return rows_of(entries, p.shape[1]).astype(BF16)


def right_features(p, marks):
    entries = [-2.0 * p[0:1], -2.0 * p[1:2], -2.0 * p[2:3], 1.0, 1.0, 1.0, *norm_parts(p), *marks]
    return rows_of(entries, p.shape[1]).astype(BF16)


def gauss(left, right, amp):
    return jnp.exp2(EXPONENT * dot(left, right, 0, 0)) * amp


def lane_index(width):
    return lax.broadcasted_iota(jnp.int32, (1, width), 1)


def chosen(attributes, index):
    spot = lax.broadcasted_iota(jnp.int32, (attributes.shape[1], index.shape[1]), 0)
    one_hot = jnp.where(spot == index, 1.0, 0.0).astype(BF16)
    return dot(attributes.astype(BF16), one_hot)


def bit_of(value, place):
    return (value >> place) & 1


def bit_of(value, place):
    return (value >> place) & 1


def describe_body(points_ref, pivots_ref, merges_ref, proj_ref, matrix_ref, merge_ref, *outs):
    given_ref, kept_ref, hi_ref, lo_ref = outs
    p = points_ref[...].astype(F32)
    width = p.shape[1]
    rank = pivots_ref.shape[1]
    levels = merge_ref.shape[0]
    position = lax.axis_index("leaf")
    spot = lane_index(width)
    attributes = rows_of(
        [p[0:1], p[1:2], p[2:3], (spot // rank).astype(F32), (spot % rank).astype(F32)], width
    )
    skeleton = chosen(attributes, pivots_ref[...])
    row = lax.broadcasted_iota(jnp.int32, skeleton.shape, 0)
    for level in range(levels - 1):
        q = merges_ref[level]
        skeleton = jnp.where(row == PIVOT + 2 * level, (q // rank).astype(F32), skeleton)
        skeleton = jnp.where(row == PIVOT + 2 * level + 1, (q % rank).astype(F32), skeleton)
    given_ref[0:HEIGHT, :] = skeleton.astype(BF16)
    c = dot(proj_ref[...], matrix_ref[...], 0, 0)
    for level in range(levels):
        hi, lo = halves(c)
        hi_ref[pl.ds(level * rank, rank), :] = hi
        lo_ref[pl.ds(level * rank, rank), :] = lo
        start = pl.multiple_of(bit_of(position, level) * rank, rank)
        m = merge_ref[level, 0, pl.ds(start, rank), :]
        c = dot(m, hi, 0, 0) + dot(m, lo, 0, 0)
    second = bit_of(position, 0) == 1
    middle = c.shape[1] // 2
    low, high = c[:, :middle], c[:, middle:]
    kept_ref[...] = jnp.where(second, high, low)
    given_ref[HEIGHT:, :] = jnp.where(second, low, high).astype(BF16)


def scatter_body(kept_ref, sent_ref, got_ref, mine_ref, *message_refs):
    chip = (lax.axis_index("leaf") >> 1) % (len(message_refs) + 1)
    count = mine_ref.shape[0]
    for k, ref in enumerate((mine_ref, *message_refs)):
        start = pl.multiple_of((chip ^ k) * count, count)
        other = got_ref[pl.ds(pl.multiple_of(HEIGHT + start, HEIGHT), count), :]
        piece = kept_ref[pl.ds(start, count), :] + other.astype(F32)
        if k == 0:
            ref[...] = piece
        else:
            ref[0:HEIGHT, :] = sent_ref[0:HEIGHT, :]
            ref[HEIGHT : 2 * HEIGHT, :] = got_ref[0:HEIGHT, :]
            ref[2 * HEIGHT :, :] = piece.astype(BF16)


def tree_body(far_amp, near_amp, even_ahead, lists_ref, *refs):
    *messages, sent_ref, got_ref, mine_ref, merges_ref, hi_ref, lo_ref, first_ref, second_ref = refs[:-4]
    top_first, top_second, part_ref, piece_ref = refs[-4:]
    piece = mine_ref[...]
    for ref in messages:
        piece += ref[2 * HEIGHT :, :].astype(F32)
    piece_ref[...] = piece.astype(BF16)
    position = lax.axis_index("leaf")
    levels = merges_ref.shape[0]
    rank = merges_ref.shape[2]
    nodes = [sent_ref[0:HEIGHT, :].astype(F32), got_ref[0:HEIGHT, :].astype(F32)]
    for ref in messages:
        nodes += [ref[0:HEIGHT, :].astype(F32), ref[HEIGHT : 2 * HEIGHT, :].astype(F32)]
    pivots = nodes
    row = lax.broadcasted_iota(jnp.int32, (HEIGHT, rank), 0)
    path = []
    for level in range(levels):
        path.append(nodes[0])
        flip = bit_of(position, level)
        merged = []
        for j in range(len(nodes) // 2):
            if level < levels - 1:
                source = pivots[j << level + 1]
                k = PIVOT + 2 * level
                q = (source[k : k + 1] * rank + source[k + 1 : k + 2]).astype(jnp.int32)
            else:
                q = merges_ref[level]
            q = jnp.where(flip == 1, jnp.where(q < rank, q + rank, q - rank), q)
            far = jnp.where(row == MEET, float(level + 1), nodes[2 * j + 1])
            merged.append(chosen(jnp.concatenate([nodes[2 * j], far], axis=1), q))
        nodes = merged
    top = nodes[0]
    blocks = lists_ref.shape[0]
    width = first_ref.shape[1]
    marks = block_marks(width, blocks)
    top_block = top[ROW_HI : ROW_HI + 1].astype(jnp.int32)
    top_here = top[MEET : MEET + 1] == 0.0
    for ref, base, near_ref in zip((first_ref, second_ref), bases_of(even_ahead, blocks), (top_first, top_second)):
        table = penalty_table(lists_ref, base, blocks)
        penalties = [
            jnp.where(top_here, per_block(top_block, [table[i][k] for i in range(blocks)]), FAR_OFF)
            for k in range(blocks)
        ]
        columns = right_features(ref[0:3, :].astype(F32), marks)
        near_ref[...] = gauss(left_features(top, penalties), columns, near_amp).astype(BF16)
    total = jnp.zeros(part_ref.shape, F32)
    for level in range(levels):
        penalty = jnp.where(top[MEET : MEET + 1] == float(level + 1), 0.0, FAR_OFF)
        block = gauss(left_features(top, [penalty]), right_features(path[level], [1.0]), -far_amp)
        block_hi, block_lo = halves(block)
        hi = hi_ref[pl.ds(level * rank, rank), :]
        lo = lo_ref[pl.ds(level * rank, rank), :]
        total += dot(block_hi, hi) + dot(block_hi, lo) + dot(block_lo, hi)
    part_ref[...] = total


def penalty_table(lists_ref, base, blocks):
    table = []
    for i in range(blocks):
        line = []
        for k in range(blocks):
            listed = lists_ref[i, 0] == base + k
            for slot in range(1, lists_ref.shape[1]):
                listed |= lists_ref[i, slot] == base + k
            line.append(jnp.where(listed, 0.0, FAR_OFF))
        table.append(line)
    return table


def per_block(block_index, values):
    out = jnp.zeros(block_index.shape, F32)
    for i, value in enumerate(values):
        out = jnp.where(block_index == i, value, out)
    return out


def block_marks(width, blocks):
    spot = lane_index(width) // (width // blocks)
    return [jnp.where(spot == k, 1.0, 0.0) for k in range(blocks)]


def bases_of(even_ahead, blocks):
    if not even_ahead:
        return [0, 2 * blocks]
    odd = lax.axis_index("blk") % 2
    return [2 * blocks * (1 - odd), 2 * blocks * odd]


def near_body(near_amp, even_ahead, lists_ref, own_ref, first_ref, second_ref, matrix_ref, *outs):
    near_first, near_second, own_terms = outs
    blocks = lists_ref.shape[0]
    own = own_ref[...].astype(F32)
    width = own.shape[1]
    spot = lane_index(width) // (width // blocks)
    marks = block_marks(width, blocks)

    def near(base, columns):
        table = penalty_table(lists_ref, base, blocks)
        penalties = [per_block(spot, [table[i][k] for i in range(blocks)]) for k in range(blocks)]
        return gauss(left_features(own, penalties), right_features(columns, marks), near_amp).astype(BF16)

    bases = bases_of(even_ahead, blocks)
    near_first[...] = near(bases[0], first_ref[0:3, :].astype(F32))
    near_second[...] = near(bases[1], second_ref[0:3, :].astype(F32))
    own_terms[...] = dot(near(blocks, own), matrix_ref[...])


def near_product(start_ref, first_ref, second_ref, *chunks):
    total = start_ref[...]
    per_side = len(chunks) // 2
    for side, left_ref in enumerate((first_ref, second_ref)):
        at = 0
        for k, chunk_ref in enumerate(chunks[side * per_side : (side + 1) * per_side]):
            lead = 0 if k else HEIGHT
            count = chunk_ref.shape[0] - lead
            total += dot(left_ref[:, at : at + count], chunk_ref[lead:, :])
            at += count
    return total


def sample_body(*refs):
    refs[-1][...] = near_product(*refs[:-1]).astype(BF16)


def share_body(*refs):
    *ins, kept_ref, given_ref = refs
    total = near_product(*ins)
    second = bit_of(lax.axis_index("leaf"), 0) == 1
    middle = total.shape[1] // 2
    low, high = total[:, :middle], total[:, middle:]
    kept_ref[...] = jnp.where(second, high, low)
    given_ref[...] = jnp.where(second, low, high).astype(BF16)


def pair_body(kept_ref, got_ref, piece_ref, out_ref):
    rank = kept_ref.shape[0]
    out_ref[0:rank, :] = (kept_ref[...] + got_ref[...].astype(F32)).astype(BF16)
    out_ref[rank:, :] = piece_ref[...]


def total_body(*refs):
    *messages, out_ref = refs
    rank = out_ref.shape[0] // 2
    count = rank // len(messages)
    chip = (lax.axis_index("leaf") >> 1) % len(messages)
    total = messages[0][0:rank, :].astype(F32)
    for ref in messages[1:]:
        total += ref[0:rank, :].astype(F32)
    out_ref[0:rank, :] = total.astype(BF16)
    for k, ref in enumerate(messages):
        start = pl.multiple_of(rank + (chip ^ k) * count, count)
        out_ref[pl.ds(start, count), :] = ref[rank:, :]


def join_body(own_ref, other_ref, samples_ref, omega_ref):
    second = bit_of(lax.axis_index("leaf"), 0) == 1
    rank, middle = samples_ref.shape[0], own_ref.shape[1]
    own, other = own_ref[...].astype(F32), other_ref[...].astype(F32)
    low, high = jnp.where(second, other, own), jnp.where(second, own, other)
    for ref, at in ((samples_ref, 0), (omega_ref, rank)):
        ref[:, :middle] = low[at : at + rank]
        ref[:, middle:] = high[at : at + rank]


def permuted(block, axis, route):
    return lax.ppermute(block, axis, [(route(i), i) for i in range(lax.axis_size(axis))])


def swapped(block, distance):
    return permuted(block, "leaf", lambda i: i ^ distance)


def on_device(points, test_matrix, near_lists, leaf_pivots, leaf_proj, merge_pivots, merge_proj):
    row_count, sample_count = test_matrix.shape
    block_count, slot_count = near_lists.shape
    skel_rank = leaf_pivots.shape[1]
    level_count = merge_pivots.shape[0]
    near_amp = 9.0 / math.sqrt(slot_count * (row_count // block_count))
    far_amp = 3.0 / math.sqrt(skel_rank)
    square = 2 * skel_rank * skel_rank * sample_count

    middle = sample_count // 2
    chips = 1 << level_count - 1
    piece = skel_rank // chips

    count = lax.axis_size("blk")
    paired = count % 2 == 0 and count > 2
    if paired:
        step = lambda i, by: (i + (by if i % 2 == 0 else -by)) % count
        routes = [lambda i: step(i, 1), lambda i: step(i, -1), lambda i: step(i, -2)]
    else:
        routes = [lambda i: (i - 1) % count, lambda i: (i + 1) % count]
    header = jnp.pad(points, ((0, HEIGHT - points.shape[0]), (0, 0)))
    chunks = [
        jnp.concatenate([header, test_matrix[: row_count // 2]], axis=0),
        test_matrix[row_count // 2 :],
    ]
    first = [permuted(c, "blk", routes[0]) for c in chunks]
    onward = list(first if paired else chunks)

    given, kept, hi, lo = call(
        describe_body,
        [((HEIGHT + skel_rank, middle), BF16), ((skel_rank, middle), F32)]
        + [((level_count * skel_rank, sample_count), BF16)] * 2,
        8 * square,
        points,
        leaf_pivots,
        merge_pivots,
        leaf_proj,
        test_matrix,
        merge_proj,
    )
    got = swapped(given, 1)
    mine, *messages = call(
        scatter_body,
        [((piece, middle), F32)] + [((2 * HEIGHT + piece, middle), BF16)] * (chips - 1),
        0,
        kept,
        given,
        got,
    )
    messages = [swapped(m, 2 * k + 2) for k, m in enumerate(messages)]
    onward[0], messages[0] = lax.optimization_barrier((onward[0], messages[0]))
    second = [permuted(onward[0], "blk", routes[-1])]
    first_points, second_points = first[0], second[0]
    near_first, near_second, own_terms = call(
        functools.partial(near_body, near_amp, paired),
        [((row_count, row_count), BF16)] * 2 + [((row_count, sample_count), F32)],
        6 * square,
        near_lists,
        points,
        first_points,
        second_points,
        test_matrix,
    )
    onward[1], messages = lax.optimization_barrier((onward[1], messages))
    second.append(permuted(onward[1], "blk", routes[-1]))
    top_first, top_second, far_part, omega_piece = call(
        functools.partial(tree_body, far_amp, near_amp, paired),
        [((skel_rank, row_count), BF16)] * 2
        + [((skel_rank, sample_count), F32), ((piece, middle), BF16)],
        9 * square,
        near_lists,
        *messages,
        given,
        got,
        mine,
        merge_pivots,
        hi,
        lo,
        first_points,
        second_points,
    )
    kept, given = call(
        share_body,
        [((skel_rank, middle), F32), ((skel_rank, middle), BF16)],
        4 * square,
        far_part,
        top_first,
        top_second,
        *first,
        *second,
    )
    got = swapped(given, 1)
    (message,) = call(pair_body, [((skel_rank + piece, middle), BF16)], 0, kept, got, omega_piece)
    messages = [message] + [swapped(message, 2 * k) for k in range(1, chips)]
    (sample,) = call(
        sample_body,
        [((row_count, sample_count), BF16)],
        8 * square,
        own_terms,
        near_first,
        near_second,
        *first,
        *second,
    )
    (total,) = call(total_body, [((2 * skel_rank, middle), BF16)], 0, *messages)
    total, sample = lax.optimization_barrier((total, sample))
    other = swapped(total, 1)
    top_samples, top_omega = call(
        join_body, [((skel_rank, sample_count), F32)] * 2, 0, total, other
    )
    return (sample, top_samples, top_omega)


def solution(mesh):
    placed = (
        P(None, ("blk", "leaf")),
        P(("blk", "leaf"), None),
        P(("blk", "leaf"), None),
        P(("blk", "leaf"), None),
        P(("blk", "leaf"), None),
        P(None, ("blk", "leaf"), None),
        P(None, ("blk", "leaf"), None, None),
    )
    return jax.shard_map(
        on_device,
        mesh=mesh,
        in_specs=placed,
        out_specs=(P(("blk", "leaf"), None), P(("blk", "leaf"), None), P(("blk", "leaf"), None)),
        check_vma=False,
    )
```

```python
import functools
import math

import jax
import jax.numpy as jnp
from jax import lax
from jax.experimental import pallas as pl
from jax.experimental.pallas import tpu as pltpu
from jax.sharding import PartitionSpec as P

SPREAD = 25.0
EXPONENT = -SPREAD * math.log2(math.e)
FAR_OFF = 1024.0
LANES = 128
HEADED = 0
HEIGHT = 16
ROW_HI, ROW_LO, MEET, PIVOT = 3, 4, 5, 6
BF16, F32 = jnp.bfloat16, jnp.float32


def call(body, outs, *args):
    return pl.pallas_call(
        body,
        out_shape=[jax.ShapeDtypeStruct(s, d) for s, d in outs],
        in_specs=[pl.BlockSpec(memory_space=pltpu.VMEM)] * len(args),
        out_specs=[pl.BlockSpec(memory_space=pltpu.VMEM)] * len(outs),
        compiler_params=pltpu.CompilerParams(vmem_limit_bytes=40 << 20),
        cost_estimate=pl.CostEstimate(flops=0, bytes_accessed=0, transcendentals=0),
    )(*args)


def dot(a, b, over_a=1, over_b=0):
    return lax.dot_general(a, b, (((over_a,), (over_b,)), ((), ())), preferred_element_type=F32)


def halves(x):
    hi = x.astype(BF16)
    return hi, (x - hi.astype(F32)).astype(BF16)


def rows_of(entries, width):
    row = lax.broadcasted_iota(jnp.int32, (HEIGHT, width), 0)
    out = jnp.zeros((HEIGHT, width), F32)
    for k, entry in enumerate(entries):
        out = jnp.where(row == k, entry, out)
    return out


def norm_parts(p):
    n = p[0:1] * p[0:1] + p[1:2] * p[1:2] + p[2:3] * p[2:3]
    hi = n.astype(BF16).astype(F32)
    mid = (n - hi).astype(BF16).astype(F32)
    return [hi, mid, n - hi - mid]


def left_features(p, penalties):
    entries = [p[0:1], p[1:2], p[2:3], *norm_parts(p), 1.0, 1.0, 1.0, *penalties]
    return rows_of(entries, p.shape[1]).astype(BF16)


def right_features(p, marks):
    entries = [-2.0 * p[0:1], -2.0 * p[1:2], -2.0 * p[2:3], 1.0, 1.0, 1.0, *norm_parts(p), *marks]
    return rows_of(entries, p.shape[1]).astype(BF16)


def gauss(left, right, amp):
    return jnp.exp2(EXPONENT * dot(left, right, 0, 0)) * amp


def lane_index(width):
    return lax.broadcasted_iota(jnp.int32, (1, width), 1)


def chosen(attributes, index):
    spot = lax.broadcasted_iota(jnp.int32, (attributes.shape[1], index.shape[1]), 0)
    one_hot = jnp.where(spot == index, 1.0, 0.0).astype(BF16)
    return dot(attributes.astype(BF16), one_hot)


def bit_of(value, place):
    return (value >> place) & 1


def bit_of(value, place):
    return (value >> place) & 1


def describe_body(*refs):
    sources, outs, held, sems = refs[:7], refs[7:13], refs[13:20], refs[20]
    given_ref, kept_ref, hi_ref, lo_ref, top_pivots_ref, table_ref = outs
    lists_ref, points_ref, pivots_ref, merges_ref, proj_ref, matrix_ref, merge_ref = held
    levels, rank = merge_ref.shape[:2]
    position = lax.axis_index("leaf")
    copies = [
        pltpu.make_async_copy(a, b, sems.at[k]) for k, (a, b) in enumerate(zip(sources[:6], held[:6]))
    ]
    for level in range(levels):
        start = pl.multiple_of(bit_of(position, level) * rank, rank)
        source = sources[6].at[level, 0, pl.ds(start, rank), :]
        copies.append(pltpu.make_async_copy(source, merge_ref.at[level], sems.at[6 + level]))
    for copy in copies:
        copy.start()
    for copy in copies[:4]:
        copy.wait()
    lists = lists_ref[...]
    blocks = lists.shape[0]
    for c in range(3 * blocks):
        listed = jnp.max(jnp.where(lists == c, 1.0, 0.0), axis=1, keepdims=True)
        for i in range(blocks):
            row = c * blocks + i
            table_ref[row : row + 1, :] = jnp.broadcast_to(FAR_OFF * (1.0 - listed[i : i + 1]), (1, LANES))
    top_pivots_ref[...] = merges_ref[merges_ref.shape[0] - 1]
    p = points_ref[...].astype(F32)
    width = p.shape[1]
    spot = lane_index(width)
    attributes = rows_of(
        [p[0:1], p[1:2], p[2:3], (spot // rank).astype(F32), (spot % rank).astype(F32)], width
    )
    skeleton = chosen(attributes, pivots_ref[...])
    row = lax.broadcasted_iota(jnp.int32, skeleton.shape, 0)
    for level in range(levels - 1):
        q = merges_ref[level]
        skeleton = jnp.where(row == PIVOT + 2 * level, (q // rank).astype(F32), skeleton)
        skeleton = jnp.where(row == PIVOT + 2 * level + 1, (q % rank).astype(F32), skeleton)
    given_ref[0:HEIGHT, :] = skeleton.astype(BF16)
    for copy in copies[4:]:
        copy.wait()
    c = dot(proj_ref[...], matrix_ref[...], 0)
    for level in range(levels):
        hi, lo = halves(c)
        hi_ref[pl.ds(level * rank, rank), :] = hi
        lo_ref[pl.ds(level * rank, rank), :] = lo
        m = merge_ref[level]
        c = dot(m, hi, 0, 0) + dot(m, lo, 0, 0)
    second = bit_of(position, 0) == 1
    middle = c.shape[1] // 2
    low, high = c[:, :middle], c[:, middle:]
    kept_ref[...] = jnp.where(second, high, low)
    given_ref[HEIGHT:, :] = jnp.where(second, low, high).astype(BF16)


def scatter_body(kept_ref, sent_ref, got_ref, mine_ref, *message_refs):
    chip = (lax.axis_index("leaf") >> 1) % (len(message_refs) + 1)
    count = mine_ref.shape[0]
    for k, ref in enumerate((mine_ref, *message_refs)):
        start = pl.multiple_of((chip ^ k) * count, count)
        other = got_ref[pl.ds(pl.multiple_of(HEIGHT + start, HEIGHT), count), :]
        piece = kept_ref[pl.ds(start, count), :] + other.astype(F32)
        if k == 0:
            ref[...] = piece
        else:
            ref[0:HEIGHT, :] = sent_ref[0:HEIGHT, :]
            ref[HEIGHT : 2 * HEIGHT, :] = got_ref[0:HEIGHT, :]
            ref[2 * HEIGHT :, :] = piece.astype(BF16)


def piece_body(*refs):
    mine_ref, *messages, out_ref = refs
    piece = mine_ref[...]
    for ref in messages:
        piece += ref[2 * HEIGHT :, :].astype(F32)
    out_ref[...] = piece.astype(BF16)


def tree_body(far_amp, *refs):
    *messages, sent_ref, got_ref, top_pivots_ref, hi_ref, lo_ref, top_ref, part_ref = refs
    position = lax.axis_index("leaf")
    rank = top_pivots_ref.shape[1]
    levels = hi_ref.shape[0] // rank
    nodes = [sent_ref[0:HEIGHT, :].astype(F32), got_ref[0:HEIGHT, :].astype(F32)]
    for ref in messages:
        nodes += [ref[0:HEIGHT, :].astype(F32), ref[HEIGHT : 2 * HEIGHT, :].astype(F32)]
    pivots = nodes
    row = lax.broadcasted_iota(jnp.int32, (HEIGHT, rank), 0)
    path = []
    for level in range(levels):
        path.append(nodes[0])
        flip = bit_of(position, level)
        merged = []
        for j in range(len(nodes) // 2):
            if level < levels - 1:
                source = pivots[j << level + 1]
                k = PIVOT + 2 * level
                q = (source[k : k + 1] * rank + source[k + 1 : k + 2]).astype(jnp.int32)
            else:
                q = top_pivots_ref[...]
            q = jnp.where(flip == 1, jnp.where(q < rank, q + rank, q - rank), q)
            far = jnp.where(row == MEET, float(level + 1), nodes[2 * j + 1])
            merged.append(chosen(jnp.concatenate([nodes[2 * j], far], axis=1), q))
        nodes = merged
    top = nodes[0]
    top_ref[...] = top
    total = jnp.zeros(part_ref.shape, F32)
    for level in range(levels):
        penalty = jnp.where(top[MEET : MEET + 1] == float(level + 1), 0.0, FAR_OFF)
        block = gauss(left_features(top, [penalty]), right_features(path[level], [1.0]), -far_amp)
        block_hi, block_lo = halves(block)
        hi = hi_ref[pl.ds(level * rank, rank), :]
        lo = lo_ref[pl.ds(level * rank, rank), :]
        total += dot(block_hi, hi) + dot(block_hi, lo) + dot(block_lo, hi)
    part_ref[...] = total


def top_near_body(near_amp, even_ahead, table_ref, top_ref, first_ref, second_ref, top_first, top_second):
    top = top_ref[...]
    blocks = block_count_of(table_ref)
    width = first_ref.shape[1]
    marks = block_marks(width, blocks)
    top_block = top[ROW_HI : ROW_HI + 1].astype(jnp.int32)
    top_here = top[MEET : MEET + 1] == 0.0
    for ref, base, near_ref in zip((first_ref, second_ref), bases_of(even_ahead, blocks), (top_first, top_second)):
        table = penalty_table(table_ref, base, blocks)
        penalties = [
            jnp.where(top_here, per_block(top_block, [table[i][k] for i in range(blocks)]), FAR_OFF)
            for k in range(blocks)
        ]
        columns = right_features(ref[0:3, :].astype(F32), marks)
        near_ref[...] = gauss(left_features(top, penalties), columns, near_amp).astype(BF16)


def block_count_of(table_ref):
    return math.isqrt(table_ref.shape[0] // 3)


def penalty_table(table_ref, base, blocks):
    return [
        [table_ref[pl.ds((base + k) * blocks + i, 1), 0:1] for k in range(blocks)] for i in range(blocks)
    ]


def per_block(block_index, values):
    out = jnp.zeros(block_index.shape, F32)
    for i, value in enumerate(values):
        out = jnp.where(block_index == i, value, out)
    return out


def block_marks(width, blocks):
    spot = lane_index(width) // (width // blocks)
    return [jnp.where(spot == k, 1.0, 0.0) for k in range(blocks)]


def bases_of(even_ahead, blocks):
    if not even_ahead:
        return [0, 2 * blocks]
    odd = lax.axis_index("blk") % 2
    return [2 * blocks * (1 - odd), 2 * blocks * odd]


def near_body(near_amp, even_ahead, table_ref, own_ref, first_ref, second_ref, matrix_ref, *outs):
    near_first, near_second, own_terms = outs
    blocks = block_count_of(table_ref)
    own = own_ref[...].astype(F32)
    width = own.shape[1]
    spot = lane_index(width) // (width // blocks)
    marks = block_marks(width, blocks)

    def near(base, columns):
        table = penalty_table(table_ref, base, blocks)
        penalties = [per_block(spot, [table[i][k] for i in range(blocks)]) for k in range(blocks)]
        return gauss(left_features(own, penalties), right_features(columns, marks), near_amp).astype(BF16)

    bases = bases_of(even_ahead, blocks)
    near_first[...] = near(bases[0], first_ref[0:3, :].astype(F32))
    near_second[...] = near(bases[1], second_ref[0:3, :].astype(F32))
    own_terms[...] = dot(near(blocks, own), matrix_ref[...])


def near_product(start_ref, first_ref, second_ref, *chunks):
    total = start_ref[...]
    per_side = len(chunks) // 2
    for side, left_ref in enumerate((first_ref, second_ref)):
        at = 0
        for k, chunk_ref in enumerate(chunks[side * per_side : (side + 1) * per_side]):
            lead = HEIGHT if k == HEADED else 0
            count = chunk_ref.shape[0] - lead
            total += dot(left_ref[:, at : at + count], chunk_ref[lead:, :])
            at += count
    return total


def sample_body(*refs):
    refs[-1][...] = near_product(*refs[:-1]).astype(BF16)


def share_body(*refs):
    *ins, kept_ref, given_ref = refs
    total = near_product(*ins)
    second = bit_of(lax.axis_index("leaf"), 0) == 1
    middle = total.shape[1] // 2
    low, high = total[:, :middle], total[:, middle:]
    kept_ref[...] = jnp.where(second, high, low)
    given_ref[...] = jnp.where(second, low, high).astype(BF16)


def pair_body(kept_ref, got_ref, out_ref):
    out_ref[...] = (kept_ref[...] + got_ref[...].astype(F32)).astype(BF16)


def total_body(*refs):
    *messages, out_ref = refs
    total = messages[0][...].astype(F32)
    for ref in messages[1:]:
        total += ref[...].astype(F32)
    out_ref[...] = total.astype(BF16)


def gather_body(*refs):
    *messages, out_ref = refs
    count = messages[0].shape[0]
    chip = (lax.axis_index("leaf") >> 1) % len(messages)
    for k, ref in enumerate(messages):
        out_ref[pl.ds(pl.multiple_of((chip ^ k) * count, count), count), :] = ref[...]


def join_body(own_ref, other_ref, out_ref):
    second = bit_of(lax.axis_index("leaf"), 0) == 1
    middle = own_ref.shape[1]
    own, other = own_ref[...].astype(F32), other_ref[...].astype(F32)
    out_ref[:, :middle] = jnp.where(second, other, own)
    out_ref[:, middle:] = jnp.where(second, own, other)


def permuted(block, axis, route):
    return lax.ppermute(block, axis, [(route(i), i) for i in range(lax.axis_size(axis))])


def swapped(block, distance):
    return permuted(block, "leaf", lambda i: i ^ distance)


def on_device(points, test_matrix, near_lists, leaf_pivots, leaf_proj, merge_pivots, merge_proj):
    row_count, sample_count = test_matrix.shape
    block_count, slot_count = near_lists.shape
    skel_rank = leaf_pivots.shape[1]
    level_count = merge_pivots.shape[0]
    near_amp = 9.0 / math.sqrt(slot_count * (row_count // block_count))
    far_amp = 3.0 / math.sqrt(skel_rank)

    middle = sample_count // 2
    chips = 1 << level_count - 1
    piece = skel_rank // chips

    count = lax.axis_size("blk")
    paired = count % 2 == 0 and count > 2
    if paired:
        step = lambda i, by: (i + (by if i % 2 == 0 else -by)) % count
        routes = [lambda i: step(i, 1), lambda i: step(i, -1), lambda i: step(i, -2)]
    else:
        routes = [lambda i: (i - 1) % count, lambda i: (i + 1) % count]
    header = jnp.pad(points, ((0, HEIGHT - points.shape[0]), (0, 0)))
    unit = row_count // 8
    edges = [0, 4 * unit, 8 * unit]
    chunks = [test_matrix[a:b] for a, b in zip(edges[:-1], edges[1:])]
    chunks[HEADED] = jnp.concatenate([header, chunks[HEADED]], axis=0)
    first = [permuted(c, "blk", routes[0]) for c in chunks]
    onward = list(first if paired else chunks)

    inputs = [near_lists, points, leaf_pivots, merge_pivots, leaf_proj, test_matrix, merge_proj]
    held = [(x.shape, x.dtype) for x in inputs[:6]] + [((level_count, skel_rank, skel_rank), BF16)]
    given, kept, hi, lo, top_pivots, table = pl.pallas_call(
        describe_body,
        out_shape=[
            jax.ShapeDtypeStruct((HEIGHT + skel_rank, middle), BF16),
            jax.ShapeDtypeStruct((skel_rank, middle), F32),
            jax.ShapeDtypeStruct((level_count * skel_rank, sample_count), BF16),
            jax.ShapeDtypeStruct((level_count * skel_rank, sample_count), BF16),
            jax.ShapeDtypeStruct((1, skel_rank), jnp.int32),
            jax.ShapeDtypeStruct((3 * block_count * block_count, LANES), F32),
        ],
        in_specs=[pl.BlockSpec(memory_space=pltpu.HBM)] * 7,
        out_specs=[pl.BlockSpec(memory_space=pltpu.VMEM)] * 6,
        scratch_shapes=[pltpu.VMEM(*h) for h in held] + [pltpu.SemaphoreType.DMA((6 + level_count,))],
        compiler_params=pltpu.CompilerParams(vmem_limit_bytes=40 << 20),
        cost_estimate=pl.CostEstimate(flops=0, bytes_accessed=0, transcendentals=0),
    )(*[pltpu.with_memory_space_constraint(x, pltpu.HBM) for x in inputs])
    got = swapped(given, 1)
    mine, *messages = call(
        scatter_body,
        [((piece, middle), F32)] + [((2 * HEIGHT + piece, middle), BF16)] * (chips - 1),
        kept,
        given,
        got,
    )
    messages = [swapped(m, 2 * k + 2) for k, m in enumerate(messages)]
    onward[0], messages[0] = lax.optimization_barrier((onward[0], messages[0]))
    second = [permuted(onward[0], "blk", routes[-1])]
    onward[1], messages = lax.optimization_barrier((onward[1], messages))
    second += [permuted(c, "blk", routes[-1]) for c in onward[1:]]
    (omega_piece,) = call(piece_body, [((piece, middle), BF16)], mine, *messages)
    omega_pieces = [omega_piece] + [swapped(omega_piece, 2 * k) for k in range(1, chips)]
    top, far_part = call(
        functools.partial(tree_body, far_amp),
        [((HEIGHT, skel_rank), F32), ((skel_rank, sample_count), F32)],
        *messages,
        given,
        got,
        top_pivots,
        hi,
        lo,
    )
    near_first, near_second, own_terms = call(
        functools.partial(near_body, near_amp, paired),
        [((row_count, row_count), BF16)] * 2 + [((row_count, sample_count), F32)],
        table,
        points,
        first[HEADED],
        second[HEADED],
        test_matrix,
    )
    top_first, top_second = call(
        functools.partial(top_near_body, near_amp, paired),
        [((skel_rank, row_count), BF16)] * 2,
        table,
        top,
        first[HEADED],
        second[HEADED],
    )
    second[-1], omega_pieces = lax.optimization_barrier((second[-1], omega_pieces))
    kept, given = call(
        share_body,
        [((skel_rank, middle), F32), ((skel_rank, middle), BF16)],
        far_part,
        top_first,
        top_second,
        *first,
        *second,
    )
    got = swapped(given, 1)
    (message,) = call(pair_body, [((skel_rank, middle), BF16)], kept, got)
    messages = [message] + [swapped(message, 2 * k) for k in range(1, chips)]
    (omega,) = call(gather_body, [((skel_rank, middle), BF16)], *omega_pieces)
    (top_omega,) = call(join_body, [((skel_rank, sample_count), F32)], omega, swapped(omega, 1))
    (sample,) = call(
        sample_body,
        [((row_count, sample_count), BF16)],
        own_terms,
        near_first,
        near_second,
        *first,
        *second,
    )
    (total,) = call(total_body, [((skel_rank, middle), BF16)], *messages)
    total, sample, top_omega = lax.optimization_barrier((total, sample, top_omega))
    (top_samples,) = call(join_body, [((skel_rank, sample_count), F32)], total, swapped(total, 1))
    return (sample, top_samples, top_omega)


def solution(mesh):
    placed = (
        P(None, ("blk", "leaf")),
        P(("blk", "leaf"), None),
        P(("blk", "leaf"), None),
        P(("blk", "leaf"), None),
        P(("blk", "leaf"), None),
        P(None, ("blk", "leaf"), None),
        P(None, ("blk", "leaf"), None, None),
    )
    return jax.shard_map(
        on_device,
        mesh=mesh,
        in_specs=placed,
        out_specs=(P(("blk", "leaf"), None), P(("blk", "leaf"), None), P(("blk", "leaf"), None)),
        check_vma=False,
    )
```

```python
import functools
import math

import jax
import jax.numpy as jnp
from jax import lax
from jax.experimental import pallas as pl
from jax.experimental.pallas import tpu as pltpu
from jax.sharding import PartitionSpec as P

SPREAD = 25.0
EXPONENT = -SPREAD * math.log2(math.e)
FAR_OFF = 1024.0
LANES = 128
HEADED = 0
HEIGHT = 16
ROW_HI, ROW_LO, MEET, PIVOT = 3, 4, 5, 6
BF16, F32 = jnp.bfloat16, jnp.float32


def call(body, outs, *args):
    return pl.pallas_call(
        body,
        out_shape=[jax.ShapeDtypeStruct(s, d) for s, d in outs],
        in_specs=[pl.BlockSpec(memory_space=pltpu.VMEM)] * len(args),
        out_specs=[pl.BlockSpec(memory_space=pltpu.VMEM)] * len(outs),
        compiler_params=pltpu.CompilerParams(vmem_limit_bytes=40 << 20),
        cost_estimate=pl.CostEstimate(flops=0, bytes_accessed=0, transcendentals=0),
    )(*args)


def dot(a, b, over_a=1, over_b=0):
    return lax.dot_general(a, b, (((over_a,), (over_b,)), ((), ())), preferred_element_type=F32)


def halves(x):
    hi = x.astype(BF16)
    return hi, (x - hi.astype(F32)).astype(BF16)


def rows_of(entries, width):
    row = lax.broadcasted_iota(jnp.int32, (HEIGHT, width), 0)
    out = jnp.zeros((HEIGHT, width), F32)
    for k, entry in enumerate(entries):
        out = jnp.where(row == k, entry, out)
    return out


def norm_parts(p):
    n = p[0:1] * p[0:1] + p[1:2] * p[1:2] + p[2:3] * p[2:3]
    hi = n.astype(BF16).astype(F32)
    mid = (n - hi).astype(BF16).astype(F32)
    return [hi, mid, n - hi - mid]


def left_features(p, penalties):
    entries = [p[0:1], p[1:2], p[2:3], *norm_parts(p), 1.0, 1.0, 1.0, *penalties]
    return rows_of(entries, p.shape[1]).astype(BF16)


def right_features(p, marks):
    entries = [-2.0 * p[0:1], -2.0 * p[1:2], -2.0 * p[2:3], 1.0, 1.0, 1.0, *norm_parts(p), *marks]
    return rows_of(entries, p.shape[1]).astype(BF16)


def gauss(left, right, amp):
    return jnp.exp2(EXPONENT * dot(left, right, 0, 0)) * amp


def lane_index(width):
    return lax.broadcasted_iota(jnp.int32, (1, width), 1)


def chosen(attributes, index):
    spot = lax.broadcasted_iota(jnp.int32, (attributes.shape[1], index.shape[1]), 0)
    one_hot = jnp.where(spot == index, 1.0, 0.0).astype(BF16)
    return dot(attributes.astype(BF16), one_hot)


def bit_of(value, place):
    return (value >> place) & 1


def bit_of(value, place):
    return (value >> place) & 1


def load_body(*refs):
    points_hbm, matrix_hbm, merge_hbm, *others = refs[:7]
    first_ref, second_ref, merge_ref, *other_refs = refs[7:14]
    points_ref, sems = refs[14:]
    position = lax.axis_index("leaf")
    levels, rank = merge_ref.shape[:2]
    rows = second_ref.shape[0]
    pairs = [
        (points_hbm, points_ref),
        (matrix_hbm.at[pl.ds(0, rows), :], first_ref.at[pl.ds(HEIGHT, rows), :]),
        (matrix_hbm.at[pl.ds(rows, rows), :], second_ref),
        *zip(others, other_refs),
    ]
    for level in range(levels):
        start = pl.multiple_of(bit_of(position, level) * rank, rank)
        pairs.append((merge_hbm.at[level, 0, pl.ds(start, rank), :], merge_ref.at[level]))
    copies = [pltpu.make_async_copy(a, b, sems.at[k]) for k, (a, b) in enumerate(pairs)]
    for copy in copies:
        copy.start()
    copies[0].wait()
    held = points_ref[...]
    blank = jnp.zeros((HEIGHT - held.shape[0], held.shape[1]), BF16)
    first_ref[0:HEIGHT, :] = jnp.concatenate([held, blank], axis=0)
    for copy in copies[1:]:
        copy.wait()


def describe_body(*refs):
    first_ref, second_ref, merge_ref, lists_ref, pivots_ref, merges_ref, proj_ref = refs[:7]
    given_ref, kept_ref, hi_ref, lo_ref, top_pivots_ref, table_ref = refs[7:]
    levels, rank = merge_ref.shape[:2]
    position = lax.axis_index("leaf")
    lists = lists_ref[...]
    blocks = lists.shape[0]
    for c in range(3 * blocks):
        listed = jnp.max(jnp.where(lists == c, 1.0, 0.0), axis=1, keepdims=True)
        for i in range(blocks):
            row = c * blocks + i
            table_ref[row : row + 1, :] = jnp.broadcast_to(FAR_OFF * (1.0 - listed[i : i + 1]), (1, LANES))
    top_pivots_ref[...] = merges_ref[merges_ref.shape[0] - 1]
    p = first_ref[0:3, :].astype(F32)
    width = p.shape[1]
    spot = lane_index(width)
    attributes = rows_of(
        [p[0:1], p[1:2], p[2:3], (spot // rank).astype(F32), (spot % rank).astype(F32)], width
    )
    skeleton = chosen(attributes, pivots_ref[...])
    row = lax.broadcasted_iota(jnp.int32, skeleton.shape, 0)
    for level in range(levels - 1):
        q = merges_ref[level]
        skeleton = jnp.where(row == PIVOT + 2 * level, (q // rank).astype(F32), skeleton)
        skeleton = jnp.where(row == PIVOT + 2 * level + 1, (q % rank).astype(F32), skeleton)
    given_ref[0:HEIGHT, :] = skeleton.astype(BF16)
    rows = second_ref.shape[0]
    c = dot(proj_ref[0:rows, :], first_ref[HEIGHT:, :], 0) + dot(proj_ref[rows:, :], second_ref[...], 0)
    for level in range(levels):
        hi, lo = halves(c)
        hi_ref[pl.ds(level * rank, rank), :] = hi
        lo_ref[pl.ds(level * rank, rank), :] = lo
        m = merge_ref[level]
        c = dot(m, hi, 0, 0) + dot(m, lo, 0, 0)
    second = bit_of(position, 0) == 1
    middle = c.shape[1] // 2
    low, high = c[:, :middle], c[:, middle:]
    kept_ref[...] = jnp.where(second, high, low)
    given_ref[HEIGHT:, :] = jnp.where(second, low, high).astype(BF16)


def scatter_body(kept_ref, sent_ref, got_ref, mine_ref, *message_refs):
    chip = (lax.axis_index("leaf") >> 1) % (len(message_refs) + 1)
    count = mine_ref.shape[0]
    for k, ref in enumerate((mine_ref, *message_refs)):
        start = pl.multiple_of((chip ^ k) * count, count)
        other = got_ref[pl.ds(pl.multiple_of(HEIGHT + start, HEIGHT), count), :]
        piece = kept_ref[pl.ds(start, count), :] + other.astype(F32)
        if k == 0:
            ref[...] = piece
        else:
            ref[0:HEIGHT, :] = sent_ref[0:HEIGHT, :]
            ref[HEIGHT : 2 * HEIGHT, :] = got_ref[0:HEIGHT, :]
            ref[2 * HEIGHT :, :] = piece.astype(BF16)


def piece_body(*refs):
    mine_ref, *messages, out_ref = refs
    piece = mine_ref[...]
    for ref in messages:
        piece += ref[2 * HEIGHT :, :].astype(F32)
    out_ref[...] = piece.astype(BF16)


def tree_body(far_amp, *refs):
    *messages, sent_ref, got_ref, top_pivots_ref, hi_ref, lo_ref, top_ref, part_ref = refs
    position = lax.axis_index("leaf")
    rank = top_pivots_ref.shape[1]
    levels = hi_ref.shape[0] // rank
    nodes = [sent_ref[0:HEIGHT, :].astype(F32), got_ref[0:HEIGHT, :].astype(F32)]
    for ref in messages:
        nodes += [ref[0:HEIGHT, :].astype(F32), ref[HEIGHT : 2 * HEIGHT, :].astype(F32)]
    pivots = nodes
    row = lax.broadcasted_iota(jnp.int32, (HEIGHT, rank), 0)
    path = []
    for level in range(levels):
        path.append(nodes[0])
        flip = bit_of(position, level)
        merged = []
        for j in range(len(nodes) // 2):
            if level < levels - 1:
                source = pivots[j << level + 1]
                k = PIVOT + 2 * level
                q = (source[k : k + 1] * rank + source[k + 1 : k + 2]).astype(jnp.int32)
            else:
                q = top_pivots_ref[...]
            q = jnp.where(flip == 1, jnp.where(q < rank, q + rank, q - rank), q)
            far = jnp.where(row == MEET, float(level + 1), nodes[2 * j + 1])
            merged.append(chosen(jnp.concatenate([nodes[2 * j], far], axis=1), q))
        nodes = merged
    top = nodes[0]
    top_ref[...] = top
    total = jnp.zeros(part_ref.shape, F32)
    for level in range(levels):
        penalty = jnp.where(top[MEET : MEET + 1] == float(level + 1), 0.0, FAR_OFF)
        block = gauss(left_features(top, [penalty]), right_features(path[level], [1.0]), -far_amp)
        block_hi, block_lo = halves(block)
        hi = hi_ref[pl.ds(level * rank, rank), :]
        lo = lo_ref[pl.ds(level * rank, rank), :]
        total += dot(block_hi, hi) + dot(block_hi, lo) + dot(block_lo, hi)
    part_ref[...] = total


def top_near_body(near_amp, even_ahead, table_ref, top_ref, first_ref, second_ref, top_first, top_second):
    top = top_ref[...]
    blocks = block_count_of(table_ref)
    width = first_ref.shape[1]
    marks = block_marks(width, blocks)
    top_block = top[ROW_HI : ROW_HI + 1].astype(jnp.int32)
    top_here = top[MEET : MEET + 1] == 0.0
    for ref, base, near_ref in zip((first_ref, second_ref), bases_of(even_ahead, blocks), (top_first, top_second)):
        table = penalty_table(table_ref, base, blocks)
        penalties = [
            jnp.where(top_here, per_block(top_block, [table[i][k] for i in range(blocks)]), FAR_OFF)
            for k in range(blocks)
        ]
        columns = right_features(ref[0:3, :].astype(F32), marks)
        near_ref[...] = gauss(left_features(top, penalties), columns, near_amp).astype(BF16)


def block_count_of(table_ref):
    return math.isqrt(table_ref.shape[0] // 3)


def penalty_table(table_ref, base, blocks):
    return [
        [table_ref[pl.ds((base + k) * blocks + i, 1), 0:1] for k in range(blocks)] for i in range(blocks)
    ]


def per_block(block_index, values):
    out = jnp.zeros(block_index.shape, F32)
    for i, value in enumerate(values):
        out = jnp.where(block_index == i, value, out)
    return out


def block_marks(width, blocks):
    spot = lane_index(width) // (width // blocks)
    return [jnp.where(spot == k, 1.0, 0.0) for k in range(blocks)]


def bases_of(even_ahead, blocks):
    if not even_ahead:
        return [0, 2 * blocks]
    odd = lax.axis_index("blk") % 2
    return [2 * blocks * (1 - odd), 2 * blocks * odd]


def near_body(near_amp, even_ahead, table_ref, first_ref, second_ref, own_ref, own_late_ref, *outs):
    near_first, near_second, own_terms = outs
    blocks = block_count_of(table_ref)
    own = own_ref[0:3, :].astype(F32)
    width = own.shape[1]
    spot = lane_index(width) // (width // blocks)
    marks = block_marks(width, blocks)

    def near(base, columns):
        table = penalty_table(table_ref, base, blocks)
        penalties = [per_block(spot, [table[i][k] for i in range(blocks)]) for k in range(blocks)]
        return gauss(left_features(own, penalties), right_features(columns, marks), near_amp).astype(BF16)

    bases = bases_of(even_ahead, blocks)
    near_first[...] = near(bases[0], first_ref[0:3, :].astype(F32))
    near_second[...] = near(bases[1], second_ref[0:3, :].astype(F32))
    near_own, rows = near(blocks, own), own_late_ref.shape[0]
    own_terms[...] = dot(near_own[:, :rows], own_ref[HEIGHT:, :]) + dot(near_own[:, rows:], own_late_ref[...])


def near_product(start_ref, first_ref, second_ref, *chunks):
    total = start_ref[...]
    per_side = len(chunks) // 2
    for side, left_ref in enumerate((first_ref, second_ref)):
        at = 0
        for k, chunk_ref in enumerate(chunks[side * per_side : (side + 1) * per_side]):
            lead = HEIGHT if k == HEADED else 0
            count = chunk_ref.shape[0] - lead
            total += dot(left_ref[:, at : at + count], chunk_ref[lead:, :])
            at += count
    return total


def sample_body(*refs):
    refs[-1][...] = near_product(*refs[:-1]).astype(BF16)


def share_body(*refs):
    *ins, kept_ref, given_ref = refs
    total = near_product(*ins)
    second = bit_of(lax.axis_index("leaf"), 0) == 1
    middle = total.shape[1] // 2
    low, high = total[:, :middle], total[:, middle:]
    kept_ref[...] = jnp.where(second, high, low)
    given_ref[...] = jnp.where(second, low, high).astype(BF16)


def pair_body(kept_ref, got_ref, out_ref):
    out_ref[...] = (kept_ref[...] + got_ref[...].astype(F32)).astype(BF16)


def total_body(*refs):
    *messages, out_ref = refs
    total = messages[0][...].astype(F32)
    for ref in messages[1:]:
        total += ref[...].astype(F32)
    out_ref[...] = total.astype(BF16)


def gather_body(*refs):
    *messages, out_ref = refs
    count = messages[0].shape[0]
    chip = (lax.axis_index("leaf") >> 1) % len(messages)
    for k, ref in enumerate(messages):
        out_ref[pl.ds(pl.multiple_of((chip ^ k) * count, count), count), :] = ref[...]


def join_body(own_ref, other_ref, out_ref):
    second = bit_of(lax.axis_index("leaf"), 0) == 1
    middle = own_ref.shape[1]
    own, other = own_ref[...].astype(F32), other_ref[...].astype(F32)
    out_ref[:, :middle] = jnp.where(second, other, own)
    out_ref[:, middle:] = jnp.where(second, own, other)


def permuted(block, axis, route):
    return lax.ppermute(block, axis, [(route(i), i) for i in range(lax.axis_size(axis))])


def swapped(block, distance):
    return permuted(block, "leaf", lambda i: i ^ distance)


def on_device(points, test_matrix, near_lists, leaf_pivots, leaf_proj, merge_pivots, merge_proj):
    row_count, sample_count = test_matrix.shape
    block_count, slot_count = near_lists.shape
    skel_rank = leaf_pivots.shape[1]
    level_count = merge_pivots.shape[0]
    near_amp = 9.0 / math.sqrt(slot_count * (row_count // block_count))
    far_amp = 3.0 / math.sqrt(skel_rank)

    middle = sample_count // 2
    chips = 1 << level_count - 1
    piece = skel_rank // chips

    count = lax.axis_size("blk")
    paired = count % 2 == 0 and count > 2
    if paired:
        step = lambda i, by: (i + (by if i % 2 == 0 else -by)) % count
        routes = [lambda i: step(i, 1), lambda i: step(i, -1), lambda i: step(i, -2)]
    else:
        routes = [lambda i: (i - 1) % count, lambda i: (i + 1) % count]
    half = row_count // 2
    inputs = [points, test_matrix, merge_proj, near_lists, leaf_pivots, merge_pivots, leaf_proj]
    loaded = pl.pallas_call(
        load_body,
        out_shape=[
            jax.ShapeDtypeStruct((HEIGHT + half, sample_count), BF16),
            jax.ShapeDtypeStruct((half, sample_count), BF16),
            jax.ShapeDtypeStruct((level_count, skel_rank, skel_rank), BF16),
        ]
        + [jax.ShapeDtypeStruct(x.shape, x.dtype) for x in inputs[3:]],
        in_specs=[pl.BlockSpec(memory_space=pltpu.HBM)] * 7,
        out_specs=[pl.BlockSpec(memory_space=pltpu.VMEM)] * 7,
        scratch_shapes=[pltpu.VMEM(points.shape, BF16), pltpu.SemaphoreType.DMA((7 + level_count,))],
        compiler_params=pltpu.CompilerParams(vmem_limit_bytes=40 << 20),
        cost_estimate=pl.CostEstimate(flops=0, bytes_accessed=0, transcendentals=0),
    )(*[pltpu.with_memory_space_constraint(x, pltpu.HBM) for x in inputs])
    chunks = loaded[:2]
    first = [permuted(c, "blk", routes[0]) for c in chunks]
    onward = list(first if paired else chunks)

    given, kept, hi, lo, top_pivots, table = call(
        describe_body,
        [((HEIGHT + skel_rank, middle), BF16), ((skel_rank, middle), F32)]
        + [((level_count * skel_rank, sample_count), BF16)] * 2
        + [((1, skel_rank), jnp.int32), ((3 * block_count * block_count, LANES), F32)],
        *loaded,
    )
    got = swapped(given, 1)
    mine, *messages = call(
        scatter_body,
        [((piece, middle), F32)] + [((2 * HEIGHT + piece, middle), BF16)] * (chips - 1),
        kept,
        given,
        got,
    )
    messages = [swapped(m, 2 * k + 2) for k, m in enumerate(messages)]
    onward[0], messages[0] = lax.optimization_barrier((onward[0], messages[0]))
    second = [permuted(onward[0], "blk", routes[-1])]
    onward[1], messages = lax.optimization_barrier((onward[1], messages))
    second += [permuted(c, "blk", routes[-1]) for c in onward[1:]]
    (omega_piece,) = call(piece_body, [((piece, middle), BF16)], mine, *messages)
    omega_pieces = [omega_piece] + [swapped(omega_piece, 2 * k) for k in range(chips - 1, 0, -1)][::-1]
    top, far_part = call(
        functools.partial(tree_body, far_amp),
        [((HEIGHT, skel_rank), F32), ((skel_rank, sample_count), F32)],
        *messages,
        given,
        got,
        top_pivots,
        hi,
        lo,
    )
    near_first, near_second, own_terms = call(
        functools.partial(near_body, near_amp, paired),
        [((row_count, row_count), BF16)] * 2 + [((row_count, sample_count), F32)],
        table,
        first[HEADED],
        second[HEADED],
        *chunks,
    )
    top_first, top_second = call(
        functools.partial(top_near_body, near_amp, paired),
        [((skel_rank, row_count), BF16)] * 2,
        table,
        top,
        first[HEADED],
        second[HEADED],
    )
    second[-1], omega_pieces = lax.optimization_barrier((second[-1], omega_pieces[::-1]))
    omega_pieces = omega_pieces[::-1]
    kept, given = call(
        share_body,
        [((skel_rank, middle), F32), ((skel_rank, middle), BF16)],
        far_part,
        top_first,
        top_second,
        *first,
        *second,
    )
    got = swapped(given, 1)
    (message,) = call(pair_body, [((skel_rank, middle), BF16)], kept, got)
    messages = [message] + [swapped(message, 2 * k) for k in range(1, chips)]
    (omega,) = call(gather_body, [((skel_rank, middle), BF16)], *omega_pieces)
    (top_omega,) = call(join_body, [((skel_rank, sample_count), F32)], omega, swapped(omega, 1))
    (sample,) = call(
        sample_body,
        [((row_count, sample_count), BF16)],
        own_terms,
        near_first,
        near_second,
        *first,
        *second,
    )
    (total,) = call(total_body, [((skel_rank, middle), BF16)], *messages)
    total, sample, top_omega = lax.optimization_barrier((total, sample, top_omega))
    (top_samples,) = call(join_body, [((skel_rank, sample_count), F32)], total, swapped(total, 1))
    return (sample, top_samples, top_omega)


def solution(mesh):
    placed = (
        P(None, ("blk", "leaf")),
        P(("blk", "leaf"), None),
        P(("blk", "leaf"), None),
        P(("blk", "leaf"), None),
        P(("blk", "leaf"), None),
        P(None, ("blk", "leaf"), None),
        P(None, ("blk", "leaf"), None, None),
    )
    return jax.shard_map(
        on_device,
        mesh=mesh,
        in_specs=placed,
        out_specs=(P(("blk", "leaf"), None), P(("blk", "leaf"), None), P(("blk", "leaf"), None)),
        check_vma=False,
    )
```

```python
import functools
import math

import jax
import jax.numpy as jnp
from jax import lax
from jax.experimental import pallas as pl
from jax.experimental.pallas import tpu as pltpu
from jax.sharding import PartitionSpec as P

SPREAD = 25.0
EXPONENT = -SPREAD * math.log2(math.e)
FAR_OFF = 1024.0
LANES = 128
HEADED = 0
HEIGHT = 16
ROW_HI, ROW_LO, MEET, PIVOT = 3, 4, 5, 6
BF16, F32 = jnp.bfloat16, jnp.float32


def call(body, outs, *args):
    return pl.pallas_call(
        body,
        out_shape=[jax.ShapeDtypeStruct(s, d) for s, d in outs],
        in_specs=[pl.BlockSpec(memory_space=pltpu.VMEM)] * len(args),
        out_specs=[pl.BlockSpec(memory_space=pltpu.VMEM)] * len(outs),
        compiler_params=pltpu.CompilerParams(vmem_limit_bytes=40 << 20),
        cost_estimate=pl.CostEstimate(flops=0, bytes_accessed=0, transcendentals=0),
    )(*args)


def dot(a, b, over_a=1, over_b=0):
    return lax.dot_general(a, b, (((over_a,), (over_b,)), ((), ())), preferred_element_type=F32)


def halves(x):
    hi = x.astype(BF16)
    return hi, (x - hi.astype(F32)).astype(BF16)


def rows_of(entries, width):
    row = lax.broadcasted_iota(jnp.int32, (HEIGHT, width), 0)
    out = jnp.zeros((HEIGHT, width), F32)
    for k, entry in enumerate(entries):
        out = jnp.where(row == k, entry, out)
    return out


def norm_parts(p):
    n = p[0:1] * p[0:1] + p[1:2] * p[1:2] + p[2:3] * p[2:3]
    hi = n.astype(BF16).astype(F32)
    mid = (n - hi).astype(BF16).astype(F32)
    return [hi, mid, n - hi - mid]


def left_features(p, penalties):
    entries = [p[0:1], p[1:2], p[2:3], *norm_parts(p), 1.0, 1.0, 1.0, *penalties]
    return rows_of(entries, p.shape[1]).astype(BF16)


def right_features(p, marks):
    entries = [-2.0 * p[0:1], -2.0 * p[1:2], -2.0 * p[2:3], 1.0, 1.0, 1.0, *norm_parts(p), *marks]
    return rows_of(entries, p.shape[1]).astype(BF16)


def gauss(left, right, amp):
    return jnp.exp2(EXPONENT * dot(left, right, 0, 0)) * amp


def lane_index(width):
    return lax.broadcasted_iota(jnp.int32, (1, width), 1)


def chosen(attributes, index):
    spot = lax.broadcasted_iota(jnp.int32, (attributes.shape[1], index.shape[1]), 0)
    one_hot = jnp.where(spot == index, 1.0, 0.0).astype(BF16)
    return dot(attributes.astype(BF16), one_hot)


def bit_of(value, place):
    return (value >> place) & 1


def bit_of(value, place):
    return (value >> place) & 1


def load_body(*refs):
    points_hbm, matrix_hbm, merge_hbm, *others = refs[:7]
    first_ref, second_ref, merge_ref, *other_refs = refs[7:14]
    points_ref, sems = refs[14:]
    position = lax.axis_index("leaf")
    levels, rank = merge_ref.shape[:2]
    rows = second_ref.shape[0]
    pairs = [
        (points_hbm, points_ref),
        (matrix_hbm.at[pl.ds(0, rows), :], first_ref.at[pl.ds(HEIGHT, rows), :]),
        (matrix_hbm.at[pl.ds(rows, rows), :], second_ref),
        *zip(others, other_refs),
    ]
    for level in range(levels):
        start = pl.multiple_of(bit_of(position, level) * rank, rank)
        pairs.append((merge_hbm.at[level, 0, pl.ds(start, rank), :], merge_ref.at[level]))
    copies = [pltpu.make_async_copy(a, b, sems.at[k]) for k, (a, b) in enumerate(pairs)]
    for copy in copies:
        copy.start()
    copies[0].wait()
    held = points_ref[...]
    blank = jnp.zeros((HEIGHT - held.shape[0], held.shape[1]), BF16)
    first_ref[0:HEIGHT, :] = jnp.concatenate([held, blank], axis=0)
    for copy in copies[1:]:
        copy.wait()


def describe_body(*refs):
    first_ref, second_ref, merge_ref, lists_ref, pivots_ref, merges_ref, proj_ref = refs[:7]
    given_ref, kept_ref, hi_ref, lo_ref, top_pivots_ref, table_ref = refs[7:]
    levels, rank = merge_ref.shape[:2]
    position = lax.axis_index("leaf")
    lists = lists_ref[...]
    blocks = lists.shape[0]
    for c in range(3 * blocks):
        listed = jnp.max(jnp.where(lists == c, 1.0, 0.0), axis=1, keepdims=True)
        for i in range(blocks):
            row = c * blocks + i
            table_ref[row : row + 1, :] = jnp.broadcast_to(FAR_OFF * (1.0 - listed[i : i + 1]), (1, LANES))
    top_pivots_ref[...] = merges_ref[merges_ref.shape[0] - 1]
    p = first_ref[0:3, :].astype(F32)
    width = p.shape[1]
    spot = lane_index(width)
    attributes = rows_of(
        [p[0:1], p[1:2], p[2:3], (spot // rank).astype(F32), (spot % rank).astype(F32)], width
    )
    skeleton = chosen(attributes, pivots_ref[...])
    row = lax.broadcasted_iota(jnp.int32, skeleton.shape, 0)
    for level in range(levels - 1):
        q = merges_ref[level]
        skeleton = jnp.where(row == PIVOT + 2 * level, (q // rank).astype(F32), skeleton)
        skeleton = jnp.where(row == PIVOT + 2 * level + 1, (q % rank).astype(F32), skeleton)
    given_ref[0:HEIGHT, :] = skeleton.astype(BF16)
    rows = second_ref.shape[0]
    c = dot(proj_ref[0:rows, :], first_ref[HEIGHT:, :], 0) + dot(proj_ref[rows:, :], second_ref[...], 0)
    for level in range(levels):
        hi, lo = halves(c)
        hi_ref[pl.ds(level * rank, rank), :] = hi
        lo_ref[pl.ds(level * rank, rank), :] = lo
        m = merge_ref[level]
        c = dot(m, hi, 0, 0) + dot(m, lo, 0, 0)
    second = bit_of(position, 0) == 1
    middle = c.shape[1] // 2
    low, high = c[:, :middle], c[:, middle:]
    kept_ref[...] = jnp.where(second, high, low)
    given_ref[HEIGHT:, :] = jnp.where(second, low, high).astype(BF16)


def scatter_body(kept_ref, sent_ref, got_ref, mine_ref, *message_refs):
    chip = (lax.axis_index("leaf") >> 1) % (len(message_refs) + 1)
    count = mine_ref.shape[0]
    for k, ref in enumerate((mine_ref, *message_refs)):
        start = pl.multiple_of((chip ^ k) * count, count)
        other = got_ref[pl.ds(pl.multiple_of(HEIGHT + start, HEIGHT), count), :]
        piece = kept_ref[pl.ds(start, count), :] + other.astype(F32)
        if k == 0:
            ref[...] = piece
        else:
            ref[0:HEIGHT, :] = sent_ref[0:HEIGHT, :]
            ref[HEIGHT : 2 * HEIGHT, :] = got_ref[0:HEIGHT, :]
            ref[2 * HEIGHT :, :] = piece.astype(BF16)


def piece_body(*refs):
    mine_ref, *messages, out_ref = refs
    piece = mine_ref[...]
    for ref in messages:
        piece += ref[2 * HEIGHT :, :].astype(F32)
    out_ref[...] = piece.astype(BF16)


def tree_body(far_amp, *refs):
    *messages, sent_ref, got_ref, top_pivots_ref, hi_ref, lo_ref, top_ref, part_ref = refs
    position = lax.axis_index("leaf")
    rank = top_pivots_ref.shape[1]
    levels = hi_ref.shape[0] // rank
    nodes = [sent_ref[0:HEIGHT, :].astype(F32), got_ref[0:HEIGHT, :].astype(F32)]
    for ref in messages:
        nodes += [ref[0:HEIGHT, :].astype(F32), ref[HEIGHT : 2 * HEIGHT, :].astype(F32)]
    pivots = nodes
    row = lax.broadcasted_iota(jnp.int32, (HEIGHT, rank), 0)
    path = []
    for level in range(levels):
        path.append(nodes[0])
        flip = bit_of(position, level)
        merged = []
        for j in range(len(nodes) // 2):
            if level < levels - 1:
                source = pivots[j << level + 1]
                k = PIVOT + 2 * level
                q = (source[k : k + 1] * rank + source[k + 1 : k + 2]).astype(jnp.int32)
            else:
                q = top_pivots_ref[...]
            q = jnp.where(flip == 1, jnp.where(q < rank, q + rank, q - rank), q)
            far = jnp.where(row == MEET, float(level + 1), nodes[2 * j + 1])
            merged.append(chosen(jnp.concatenate([nodes[2 * j], far], axis=1), q))
        nodes = merged
    top = nodes[0]
    top_ref[...] = top
    total = jnp.zeros(part_ref.shape, F32)
    for level in range(levels):
        penalty = jnp.where(top[MEET : MEET + 1] == float(level + 1), 0.0, FAR_OFF)
        block = gauss(left_features(top, [penalty]), right_features(path[level], [1.0]), -far_amp)
        block_hi, block_lo = halves(block)
        hi = hi_ref[pl.ds(level * rank, rank), :]
        lo = lo_ref[pl.ds(level * rank, rank), :]
        total += dot(block_hi, hi) + dot(block_hi, lo) + dot(block_lo, hi)
    part_ref[...] = total


def top_near_body(near_amp, even_ahead, table_ref, top_ref, first_ref, second_ref, top_first, top_second):
    top = top_ref[...]
    blocks = block_count_of(table_ref)
    width = first_ref.shape[1]
    marks = block_marks(width, blocks)
    top_block = top[ROW_HI : ROW_HI + 1].astype(jnp.int32)
    top_here = top[MEET : MEET + 1] == 0.0
    for ref, base, near_ref in zip((first_ref, second_ref), bases_of(even_ahead, blocks), (top_first, top_second)):
        table = penalty_table(table_ref, base, blocks)
        penalties = [
            jnp.where(top_here, per_block(top_block, [table[i][k] for i in range(blocks)]), FAR_OFF)
            for k in range(blocks)
        ]
        columns = right_features(ref[0:3, :].astype(F32), marks)
        near_ref[...] = gauss(left_features(top, penalties), columns, near_amp).astype(BF16)


def block_count_of(table_ref):
    return math.isqrt(table_ref.shape[0] // 3)


def penalty_table(table_ref, base, blocks):
    return [
        [table_ref[pl.ds((base + k) * blocks + i, 1), 0:1] for k in range(blocks)] for i in range(blocks)
    ]


def per_block(block_index, values):
    out = jnp.zeros(block_index.shape, F32)
    for i, value in enumerate(values):
        out = jnp.where(block_index == i, value, out)
    return out


def block_marks(width, blocks):
    spot = lane_index(width) // (width // blocks)
    return [jnp.where(spot == k, 1.0, 0.0) for k in range(blocks)]


def bases_of(even_ahead, blocks):
    if not even_ahead:
        return [0, 2 * blocks]
    odd = lax.axis_index("blk") % 2
    return [2 * blocks * (1 - odd), 2 * blocks * odd]


def near_body(near_amp, even_ahead, table_ref, first_ref, second_ref, own_ref, own_late_ref, *outs):
    near_first, near_second, own_terms = outs
    blocks = block_count_of(table_ref)
    own = own_ref[0:3, :].astype(F32)
    width = own.shape[1]
    spot = lane_index(width) // (width // blocks)
    marks = block_marks(width, blocks)

    def near(base, columns):
        table = penalty_table(table_ref, base, blocks)
        penalties = [per_block(spot, [table[i][k] for i in range(blocks)]) for k in range(blocks)]
        return gauss(left_features(own, penalties), right_features(columns, marks), near_amp).astype(BF16)

    bases = bases_of(even_ahead, blocks)
    near_first[...] = near(bases[0], first_ref[0:3, :].astype(F32))
    near_second[...] = near(bases[1], second_ref[0:3, :].astype(F32))
    near_own, rows = near(blocks, own), own_late_ref.shape[0]
    own_terms[...] = dot(near_own[:, :rows], own_ref[HEIGHT:, :]) + dot(near_own[:, rows:], own_late_ref[...])


def near_product(start_ref, first_ref, second_ref, *chunks):
    total = start_ref[...]
    per_side = len(chunks) // 2
    for side, left_ref in enumerate((first_ref, second_ref)):
        at = 0
        for k, chunk_ref in enumerate(chunks[side * per_side : (side + 1) * per_side]):
            lead = HEIGHT if k == HEADED else 0
            count = chunk_ref.shape[0] - lead
            total += dot(left_ref[:, at : at + count], chunk_ref[lead:, :])
            at += count
    return total


def sample_body(*refs):
    refs[-1][...] = near_product(*refs[:-1]).astype(BF16)


def share_body(*refs):
    *ins, kept_ref, given_ref = refs
    total = near_product(*ins)
    second = bit_of(lax.axis_index("leaf"), 0) == 1
    middle = total.shape[1] // 2
    low, high = total[:, :middle], total[:, middle:]
    kept_ref[...] = jnp.where(second, high, low)
    given_ref[...] = jnp.where(second, low, high).astype(BF16)


def pair_body(kept_ref, got_ref, out_ref):
    out_ref[...] = (kept_ref[...] + got_ref[...].astype(F32)).astype(BF16)


def total_body(*refs):
    *messages, out_ref = refs
    total = messages[0][...].astype(F32)
    for ref in messages[1:]:
        total += ref[...].astype(F32)
    out_ref[...] = total.astype(BF16)


def gather_body(*refs):
    *messages, out_ref = refs
    count = messages[0].shape[0]
    chip = (lax.axis_index("leaf") >> 1) % len(messages)
    for k, ref in enumerate(messages):
        out_ref[pl.ds(pl.multiple_of((chip ^ k) * count, count), count), :] = ref[...]


def join_body(own_ref, other_ref, out_ref):
    second = bit_of(lax.axis_index("leaf"), 0) == 1
    middle = own_ref.shape[1]
    own, other = own_ref[...].astype(F32), other_ref[...].astype(F32)
    out_ref[:, :middle] = jnp.where(second, other, own)
    out_ref[:, middle:] = jnp.where(second, own, other)


def permuted(block, axis, route):
    return lax.ppermute(block, axis, [(route(i), i) for i in range(lax.axis_size(axis))])


def swapped(block, distance):
    return permuted(block, "leaf", lambda i: i ^ distance)


def on_device(points, test_matrix, near_lists, leaf_pivots, leaf_proj, merge_pivots, merge_proj):
    row_count, sample_count = test_matrix.shape
    block_count, slot_count = near_lists.shape
    skel_rank = leaf_pivots.shape[1]
    level_count = merge_pivots.shape[0]
    near_amp = 9.0 / math.sqrt(slot_count * (row_count // block_count))
    far_amp = 3.0 / math.sqrt(skel_rank)

    middle = sample_count // 2
    chips = 1 << level_count - 1
    piece = skel_rank // chips

    count = lax.axis_size("blk")
    paired = count % 2 == 0 and count > 2
    if paired:
        step = lambda i, by: (i + (by if i % 2 == 0 else -by)) % count
        routes = [lambda i: step(i, 1), lambda i: step(i, -1), lambda i: step(i, -2)]
    else:
        routes = [lambda i: (i - 1) % count, lambda i: (i + 1) % count]
    half = row_count // 2
    inputs = [points, test_matrix, merge_proj, near_lists, leaf_pivots, merge_pivots, leaf_proj]
    loaded = pl.pallas_call(
        load_body,
        out_shape=[
            jax.ShapeDtypeStruct((HEIGHT + half, sample_count), BF16),
            jax.ShapeDtypeStruct((half, sample_count), BF16),
            jax.ShapeDtypeStruct((level_count, skel_rank, skel_rank), BF16),
        ]
        + [jax.ShapeDtypeStruct(x.shape, x.dtype) for x in inputs[3:]],
        in_specs=[pl.BlockSpec(memory_space=pltpu.HBM)] * 7,
        out_specs=[pl.BlockSpec(memory_space=pltpu.VMEM)] * 7,
        scratch_shapes=[pltpu.VMEM(points.shape, BF16), pltpu.SemaphoreType.DMA((7 + level_count,))],
        compiler_params=pltpu.CompilerParams(vmem_limit_bytes=40 << 20),
        cost_estimate=pl.CostEstimate(flops=0, bytes_accessed=0, transcendentals=0),
    )(*[pltpu.with_memory_space_constraint(x, pltpu.HBM) for x in inputs])
    chunks = loaded[:2]
    first = [permuted(c, "blk", routes[0]) for c in chunks]
    onward = list(first if paired else chunks)

    given, kept, hi, lo, top_pivots, table = call(
        describe_body,
        [((HEIGHT + skel_rank, middle), BF16), ((skel_rank, middle), F32)]
        + [((level_count * skel_rank, sample_count), BF16)] * 2
        + [((1, skel_rank), jnp.int32), ((3 * block_count * block_count, LANES), F32)],
        *loaded,
    )
    got = swapped(given, 1)
    mine, *messages = call(
        scatter_body,
        [((piece, middle), F32)] + [((2 * HEIGHT + piece, middle), BF16)] * (chips - 1),
        kept,
        given,
        got,
    )
    messages = [swapped(m, 2 * k + 2) for k, m in enumerate(messages)]
    onward[0], messages[0] = lax.optimization_barrier((onward[0], messages[0]))
    second = [permuted(onward[0], "blk", routes[-1])]
    order = sorted(range(1, chips), key=lambda k: (k < 2, k))
    onward[1], messages = lax.optimization_barrier((onward[1], messages))
    second += [permuted(c, "blk", routes[-1]) for c in onward[1:]]
    (omega_piece,) = call(piece_body, [((piece, middle), BF16)], mine, *messages)
    omega_pieces = [omega_piece] + [swapped(omega_piece, 2 * k) for k in range(chips - 1, 0, -1)][::-1]
    top, far_part = call(
        functools.partial(tree_body, far_amp),
        [((HEIGHT, skel_rank), F32), ((skel_rank, sample_count), F32)],
        *messages,
        given,
        got,
        top_pivots,
        hi,
        lo,
    )
    near_first, near_second, own_terms = call(
        functools.partial(near_body, near_amp, paired),
        [((row_count, row_count), BF16)] * 2 + [((row_count, sample_count), F32)],
        table,
        first[HEADED],
        second[HEADED],
        *chunks,
    )
    top_first, top_second = call(
        functools.partial(top_near_body, near_amp, paired),
        [((skel_rank, row_count), BF16)] * 2,
        table,
        top,
        first[HEADED],
        second[HEADED],
    )
    second[-1], held = lax.optimization_barrier((second[-1], [omega_pieces[k] for k in order]))
    omega_pieces[1:] = [held[order.index(k)] for k in range(1, chips)]
    kept, given = call(
        share_body,
        [((skel_rank, middle), F32), ((skel_rank, middle), BF16)],
        far_part,
        top_first,
        top_second,
        *first,
        *second,
    )
    got = swapped(given, 1)
    (message,) = call(pair_body, [((skel_rank, middle), BF16)], kept, got)
    messages = [message] + [swapped(message, 2 * k) for k in range(1, chips)]
    (omega,) = call(gather_body, [((skel_rank, middle), BF16)], *omega_pieces)
    (top_omega,) = call(join_body, [((skel_rank, sample_count), F32)], omega, swapped(omega, 1))
    (sample,) = call(
        sample_body,
        [((row_count, sample_count), BF16)],
        own_terms,
        near_first,
        near_second,
        *first,
        *second,
    )
    messages = [messages[k] for k in sorted(range(chips), key=lambda k: (k % 2, k))]
    (total,) = call(total_body, [((skel_rank, middle), BF16)], *messages)
    total, sample, top_omega = lax.optimization_barrier((total, sample, top_omega))
    (top_samples,) = call(join_body, [((skel_rank, sample_count), F32)], total, swapped(total, 1))
    return (sample, top_samples, top_omega)


def solution(mesh):
    placed = (
        P(None, ("blk", "leaf")),
        P(("blk", "leaf"), None),
        P(("blk", "leaf"), None),
        P(("blk", "leaf"), None),
        P(("blk", "leaf"), None),
        P(None, ("blk", "leaf"), None),
        P(None, ("blk", "leaf"), None, None),
    )
    return jax.shard_map(
        on_device,
        mesh=mesh,
        in_specs=placed,
        out_specs=(P(("blk", "leaf"), None), P(("blk", "leaf"), None), P(("blk", "leaf"), None)),
        check_vma=False,
    )
```

```python
import functools
import math

import jax
import jax.numpy as jnp
from jax import lax
from jax.experimental import pallas as pl
from jax.experimental.pallas import tpu as pltpu
from jax.sharding import PartitionSpec as P

SPREAD = 25.0
EXPONENT = -SPREAD * math.log2(math.e)
FAR_OFF = 1024.0
LANES = 128
HEADED = 0
HEIGHT = 16
ROW_HI, ROW_LO, MEET, PIVOT = 3, 4, 5, 6
BF16, F32 = jnp.bfloat16, jnp.float32


def call(body, outs, *args):
    return pl.pallas_call(
        body,
        out_shape=[jax.ShapeDtypeStruct(s, d) for s, d in outs],
        in_specs=[pl.BlockSpec(memory_space=pltpu.VMEM)] * len(args),
        out_specs=[pl.BlockSpec(memory_space=pltpu.VMEM)] * len(outs),
        compiler_params=pltpu.CompilerParams(vmem_limit_bytes=40 << 20),
        cost_estimate=pl.CostEstimate(flops=0, bytes_accessed=0, transcendentals=0),
    )(*args)


def dot(a, b, over_a=1, over_b=0):
    return lax.dot_general(a, b, (((over_a,), (over_b,)), ((), ())), preferred_element_type=F32)


def halves(x):
    hi = x.astype(BF16)
    return hi, (x - hi.astype(F32)).astype(BF16)


def rows_of(entries, width):
    row = lax.broadcasted_iota(jnp.int32, (HEIGHT, width), 0)
    out = jnp.zeros((HEIGHT, width), F32)
    for k, entry in enumerate(entries):
        out = jnp.where(row == k, entry, out)
    return out


def norm_parts(p):
    n = p[0:1] * p[0:1] + p[1:2] * p[1:2] + p[2:3] * p[2:3]
    hi = n.astype(BF16).astype(F32)
    mid = (n - hi).astype(BF16).astype(F32)
    return [hi, mid, n - hi - mid]


def left_features(p, penalties):
    entries = [p[0:1], p[1:2], p[2:3], *norm_parts(p), 1.0, 1.0, 1.0, *penalties]
    return rows_of(entries, p.shape[1]).astype(BF16)


def right_features(p, marks):
    entries = [-2.0 * p[0:1], -2.0 * p[1:2], -2.0 * p[2:3], 1.0, 1.0, 1.0, *norm_parts(p), *marks]
    return rows_of(entries, p.shape[1]).astype(BF16)


def gauss(left, right, amp):
    return jnp.exp2(EXPONENT * dot(left, right, 0, 0)) * amp


def lane_index(width):
    return lax.broadcasted_iota(jnp.int32, (1, width), 1)


def chosen(attributes, index):
    spot = lax.broadcasted_iota(jnp.int32, (attributes.shape[1], index.shape[1]), 0)
    one_hot = jnp.where(spot == index, 1.0, 0.0).astype(BF16)
    return dot(attributes.astype(BF16), one_hot)


def bit_of(value, place):
    return (value >> place) & 1


def bit_of(value, place):
    return (value >> place) & 1


def load_body(*refs):
    points_hbm, matrix_hbm, merge_hbm, *others = refs[:7]
    first_ref, second_ref, merge_ref, *other_refs = refs[7:14]
    points_ref, sems = refs[14:]
    position = lax.axis_index("leaf")
    levels, rank = merge_ref.shape[:2]
    rows = second_ref.shape[0]
    pairs = [
        (points_hbm, points_ref),
        (matrix_hbm.at[pl.ds(0, rows), :], first_ref.at[pl.ds(HEIGHT, rows), :]),
        (matrix_hbm.at[pl.ds(rows, rows), :], second_ref),
        *zip(others, other_refs),
    ]
    for level in range(levels):
        start = pl.multiple_of(bit_of(position, level) * rank, rank)
        pairs.append((merge_hbm.at[level, 0, pl.ds(start, rank), :], merge_ref.at[level]))
    copies = [pltpu.make_async_copy(a, b, sems.at[k]) for k, (a, b) in enumerate(pairs)]
    for copy in copies:
        copy.start()
    copies[0].wait()
    held = points_ref[...]
    blank = jnp.zeros((HEIGHT - held.shape[0], held.shape[1]), BF16)
    first_ref[0:HEIGHT, :] = jnp.concatenate([held, blank], axis=0)
    for copy in copies[1:]:
        copy.wait()


def describe_body(*refs):
    first_ref, second_ref, merge_ref, lists_ref, pivots_ref, merges_ref, proj_ref = refs[:7]
    given_ref, kept_ref, hi_ref, lo_ref, top_pivots_ref, table_ref = refs[7:]
    levels, rank = merge_ref.shape[:2]
    position = lax.axis_index("leaf")
    lists = lists_ref[...]
    blocks = lists.shape[0]
    for c in range(3 * blocks):
        listed = jnp.max(jnp.where(lists == c, 1.0, 0.0), axis=1, keepdims=True)
        for i in range(blocks):
            row = c * blocks + i
            table_ref[row : row + 1, :] = jnp.broadcast_to(FAR_OFF * (1.0 - listed[i : i + 1]), (1, LANES))
    top_pivots_ref[...] = merges_ref[merges_ref.shape[0] - 1]
    p = first_ref[0:3, :].astype(F32)
    width = p.shape[1]
    spot = lane_index(width)
    attributes = rows_of(
        [p[0:1], p[1:2], p[2:3], (spot // rank).astype(F32), (spot % rank).astype(F32)], width
    )
    skeleton = chosen(attributes, pivots_ref[...])
    row = lax.broadcasted_iota(jnp.int32, skeleton.shape, 0)
    for level in range(levels - 1):
        q = merges_ref[level]
        skeleton = jnp.where(row == PIVOT + 2 * level, (q // rank).astype(F32), skeleton)
        skeleton = jnp.where(row == PIVOT + 2 * level + 1, (q % rank).astype(F32), skeleton)
    given_ref[0:HEIGHT, :] = skeleton.astype(BF16)
    rows = second_ref.shape[0]
    c = dot(proj_ref[0:rows, :], first_ref[HEIGHT:, :], 0) + dot(proj_ref[rows:, :], second_ref[...], 0)
    for level in range(levels):
        hi, lo = halves(c)
        hi_ref[pl.ds(level * rank, rank), :] = hi
        lo_ref[pl.ds(level * rank, rank), :] = lo
        m = merge_ref[level]
        c = dot(m, hi, 0, 0) + dot(m, lo, 0, 0)
    second = bit_of(position, 0) == 1
    middle = c.shape[1] // 2
    low, high = c[:, :middle], c[:, middle:]
    kept_ref[...] = jnp.where(second, high, low)
    given_ref[HEIGHT:, :] = jnp.where(second, low, high).astype(BF16)


def scatter_body(kept_ref, sent_ref, got_ref, mine_ref, *message_refs):
    chip = (lax.axis_index("leaf") >> 1) % (len(message_refs) + 1)
    count = mine_ref.shape[0]
    for k, ref in enumerate((mine_ref, *message_refs)):
        start = pl.multiple_of((chip ^ k) * count, count)
        other = got_ref[pl.ds(pl.multiple_of(HEIGHT + start, HEIGHT), count), :]
        piece = kept_ref[pl.ds(start, count), :] + other.astype(F32)
        if k == 0:
            ref[...] = piece
        else:
            ref[0:HEIGHT, :] = sent_ref[0:HEIGHT, :]
            ref[HEIGHT : 2 * HEIGHT, :] = got_ref[0:HEIGHT, :]
            ref[2 * HEIGHT :, :] = piece.astype(BF16)


def piece_body(*refs):
    mine_ref, *messages, out_ref = refs
    piece = mine_ref[...]
    for ref in messages:
        piece += ref[2 * HEIGHT :, :].astype(F32)
    out_ref[...] = piece.astype(BF16)


def tree_body(far_amp, *refs):
    *messages, sent_ref, got_ref, top_pivots_ref, hi_ref, lo_ref, top_ref, part_ref = refs
    position = lax.axis_index("leaf")
    rank = top_pivots_ref.shape[1]
    levels = hi_ref.shape[0] // rank
    nodes = [sent_ref[0:HEIGHT, :].astype(F32), got_ref[0:HEIGHT, :].astype(F32)]
    for ref in messages:
        nodes += [ref[0:HEIGHT, :].astype(F32), ref[HEIGHT : 2 * HEIGHT, :].astype(F32)]
    pivots = nodes
    row = lax.broadcasted_iota(jnp.int32, (HEIGHT, rank), 0)
    path = []
    for level in range(levels):
        path.append(nodes[0])
        flip = bit_of(position, level)
        merged = []
        for j in range(len(nodes) // 2):
            if level < levels - 1:
                source = pivots[j << level + 1]
                k = PIVOT + 2 * level
                q = (source[k : k + 1] * rank + source[k + 1 : k + 2]).astype(jnp.int32)
            else:
                q = top_pivots_ref[...]
            q = jnp.where(flip == 1, jnp.where(q < rank, q + rank, q - rank), q)
            far = jnp.where(row == MEET, float(level + 1), nodes[2 * j + 1])
            merged.append(chosen(jnp.concatenate([nodes[2 * j], far], axis=1), q))
        nodes = merged
    top = nodes[0]
    top_ref[...] = top
    total = jnp.zeros(part_ref.shape, F32)
    for level in range(levels):
        penalty = jnp.where(top[MEET : MEET + 1] == float(level + 1), 0.0, FAR_OFF)
        block = gauss(left_features(top, [penalty]), right_features(path[level], [1.0]), -far_amp)
        block_hi, block_lo = halves(block)
        hi = hi_ref[pl.ds(level * rank, rank), :]
        lo = lo_ref[pl.ds(level * rank, rank), :]
        total += dot(block_hi, hi) + dot(block_hi, lo) + dot(block_lo, hi)
    part_ref[...] = total


def top_near_body(near_amp, even_ahead, table_ref, top_ref, first_ref, second_ref, top_first, top_second):
    top = top_ref[...]
    blocks = block_count_of(table_ref)
    width = first_ref.shape[1]
    marks = block_marks(width, blocks)
    top_block = top[ROW_HI : ROW_HI + 1].astype(jnp.int32)
    top_here = top[MEET : MEET + 1] == 0.0
    for ref, base, near_ref in zip((first_ref, second_ref), bases_of(even_ahead, blocks), (top_first, top_second)):
        table = penalty_table(table_ref, base, blocks)
        penalties = [
            jnp.where(top_here, per_block(top_block, [table[i][k] for i in range(blocks)]), FAR_OFF)
            for k in range(blocks)
        ]
        columns = right_features(ref[0:3, :].astype(F32), marks)
        near_ref[...] = gauss(left_features(top, penalties), columns, near_amp).astype(BF16)


def block_count_of(table_ref):
    return math.isqrt(table_ref.shape[0] // 3)


def penalty_table(table_ref, base, blocks):
    return [
        [table_ref[pl.ds((base + k) * blocks + i, 1), 0:1] for k in range(blocks)] for i in range(blocks)
    ]


def per_block(block_index, values):
    out = jnp.zeros(block_index.shape, F32)
    for i, value in enumerate(values):
        out = jnp.where(block_index == i, value, out)
    return out


def block_marks(width, blocks):
    spot = lane_index(width) // (width // blocks)
    return [jnp.where(spot == k, 1.0, 0.0) for k in range(blocks)]


def bases_of(even_ahead, blocks):
    if not even_ahead:
        return [0, 2 * blocks]
    odd = lax.axis_index("blk") % 2
    return [2 * blocks * (1 - odd), 2 * blocks * odd]


def near_body(near_amp, even_ahead, table_ref, first_ref, second_ref, own_ref, own_late_ref, *outs):
    near_first, near_second, own_terms = outs
    blocks = block_count_of(table_ref)
    own = own_ref[0:3, :].astype(F32)
    width = own.shape[1]
    spot = lane_index(width) // (width // blocks)
    marks = block_marks(width, blocks)

    def near(base, columns):
        table = penalty_table(table_ref, base, blocks)
        penalties = [per_block(spot, [table[i][k] for i in range(blocks)]) for k in range(blocks)]
        return gauss(left_features(own, penalties), right_features(columns, marks), near_amp).astype(BF16)

    bases = bases_of(even_ahead, blocks)
    near_first[...] = near(bases[0], first_ref[0:3, :].astype(F32))
    near_second[...] = near(bases[1], second_ref[0:3, :].astype(F32))
    near_own, rows = near(blocks, own), own_late_ref.shape[0]
    own_terms[...] = dot(near_own[:, :rows], own_ref[HEIGHT:, :]) + dot(near_own[:, rows:], own_late_ref[...])


def near_product(start_ref, first_ref, second_ref, *chunks):
    total = start_ref[...]
    per_side = len(chunks) // 2
    for side, left_ref in enumerate((first_ref, second_ref)):
        at = 0
        for k, chunk_ref in enumerate(chunks[side * per_side : (side + 1) * per_side]):
            lead = HEIGHT if k == HEADED else 0
            count = chunk_ref.shape[0] - lead
            total += dot(left_ref[:, at : at + count], chunk_ref[lead:, :])
            at += count
    return total


def sample_body(*refs):
    refs[-1][...] = near_product(*refs[:-1]).astype(BF16)


def partial_body(start_ref, first_ref, second_ref, early_ref, late_ref, upper_ref, out_ref):
    cut = early_ref.shape[0] - HEIGHT
    total = start_ref[...] + dot(first_ref[:, :cut], early_ref[HEIGHT:, :])
    total += dot(first_ref[:, cut:], late_ref[...])
    out_ref[...] = total + dot(second_ref[:, :cut], upper_ref[HEIGHT:, :])


def share_body(start_ref, second_ref, lower_ref, kept_ref, given_ref):
    cut = second_ref.shape[1] - lower_ref.shape[0]
    total = start_ref[...] + dot(second_ref[:, cut:], lower_ref[...])
    second = bit_of(lax.axis_index("leaf"), 0) == 1
    middle = total.shape[1] // 2
    low, high = total[:, :middle], total[:, middle:]
    kept_ref[...] = jnp.where(second, high, low)
    given_ref[...] = jnp.where(second, low, high).astype(BF16)


def pair_body(kept_ref, got_ref, out_ref):
    out_ref[...] = (kept_ref[...] + got_ref[...].astype(F32)).astype(BF16)


def total_body(*refs):
    *messages, out_ref = refs
    total = messages[0][...].astype(F32)
    for ref in messages[1:]:
        total += ref[...].astype(F32)
    out_ref[...] = total.astype(BF16)


def gather_body(*refs):
    *messages, out_ref = refs
    count = messages[0].shape[0]
    chip = (lax.axis_index("leaf") >> 1) % len(messages)
    for k, ref in enumerate(messages):
        out_ref[pl.ds(pl.multiple_of((chip ^ k) * count, count), count), :] = ref[...]


def join_body(own_ref, other_ref, out_ref):
    second = bit_of(lax.axis_index("leaf"), 0) == 1
    middle = own_ref.shape[1]
    own, other = own_ref[...].astype(F32), other_ref[...].astype(F32)
    out_ref[:, :middle] = jnp.where(second, other, own)
    out_ref[:, middle:] = jnp.where(second, own, other)


def permuted(block, axis, route):
    return lax.ppermute(block, axis, [(route(i), i) for i in range(lax.axis_size(axis))])


def swapped(block, distance):
    return permuted(block, "leaf", lambda i: i ^ distance)


def on_device(points, test_matrix, near_lists, leaf_pivots, leaf_proj, merge_pivots, merge_proj):
    row_count, sample_count = test_matrix.shape
    block_count, slot_count = near_lists.shape
    skel_rank = leaf_pivots.shape[1]
    level_count = merge_pivots.shape[0]
    near_amp = 9.0 / math.sqrt(slot_count * (row_count // block_count))
    far_amp = 3.0 / math.sqrt(skel_rank)

    middle = sample_count // 2
    chips = 1 << level_count - 1
    piece = skel_rank // chips

    count = lax.axis_size("blk")
    paired = count % 2 == 0 and count > 2
    if paired:
        step = lambda i, by: (i + (by if i % 2 == 0 else -by)) % count
        routes = [lambda i: step(i, 1), lambda i: step(i, -1), lambda i: step(i, -2)]
    else:
        routes = [lambda i: (i - 1) % count, lambda i: (i + 1) % count]
    half = row_count // 2
    inputs = [points, test_matrix, merge_proj, near_lists, leaf_pivots, merge_pivots, leaf_proj]
    loaded = pl.pallas_call(
        load_body,
        out_shape=[
            jax.ShapeDtypeStruct((HEIGHT + half, sample_count), BF16),
            jax.ShapeDtypeStruct((half, sample_count), BF16),
            jax.ShapeDtypeStruct((level_count, skel_rank, skel_rank), BF16),
        ]
        + [jax.ShapeDtypeStruct(x.shape, x.dtype) for x in inputs[3:]],
        in_specs=[pl.BlockSpec(memory_space=pltpu.HBM)] * 7,
        out_specs=[pl.BlockSpec(memory_space=pltpu.VMEM)] * 7,
        scratch_shapes=[pltpu.VMEM(points.shape, BF16), pltpu.SemaphoreType.DMA((7 + level_count,))],
        compiler_params=pltpu.CompilerParams(vmem_limit_bytes=40 << 20),
        cost_estimate=pl.CostEstimate(flops=0, bytes_accessed=0, transcendentals=0),
    )(*[pltpu.with_memory_space_constraint(x, pltpu.HBM) for x in inputs])
    chunks = loaded[:2]
    first = [permuted(c, "blk", routes[0]) for c in chunks]
    onward = list(first if paired else chunks)

    given, kept, hi, lo, top_pivots, table = call(
        describe_body,
        [((HEIGHT + skel_rank, middle), BF16), ((skel_rank, middle), F32)]
        + [((level_count * skel_rank, sample_count), BF16)] * 2
        + [((1, skel_rank), jnp.int32), ((3 * block_count * block_count, LANES), F32)],
        *loaded,
    )
    got = swapped(given, 1)
    mine, *messages = call(
        scatter_body,
        [((piece, middle), F32)] + [((2 * HEIGHT + piece, middle), BF16)] * (chips - 1),
        kept,
        given,
        got,
    )
    messages = [swapped(m, 2 * k + 2) for k, m in enumerate(messages)]
    onward[0], messages[0] = lax.optimization_barrier((onward[0], messages[0]))
    second = [permuted(onward[0], "blk", routes[-1])]
    order = sorted(range(1, chips), key=lambda k: (k < 2, k))
    onward[1], messages = lax.optimization_barrier((onward[1], messages))
    second += [permuted(c, "blk", routes[-1]) for c in onward[1:]]
    (omega_piece,) = call(piece_body, [((piece, middle), BF16)], mine, *messages)
    omega_pieces = [omega_piece] + [swapped(omega_piece, 2 * k) for k in range(chips - 1, 0, -1)][::-1]
    top, far_part = call(
        functools.partial(tree_body, far_amp),
        [((HEIGHT, skel_rank), F32), ((skel_rank, sample_count), F32)],
        *messages,
        given,
        got,
        top_pivots,
        hi,
        lo,
    )
    near_first, near_second, own_terms = call(
        functools.partial(near_body, near_amp, paired),
        [((row_count, row_count), BF16)] * 2 + [((row_count, sample_count), F32)],
        table,
        first[HEADED],
        second[HEADED],
        *chunks,
    )
    top_first, top_second = call(
        functools.partial(top_near_body, near_amp, paired),
        [((skel_rank, row_count), BF16)] * 2,
        table,
        top,
        first[HEADED],
        second[HEADED],
    )
    (partial,) = call(
        partial_body, [((skel_rank, sample_count), F32)], far_part, top_first, top_second, *first, second[0]
    )
    second[-1], held = lax.optimization_barrier((second[-1], [omega_pieces[k] for k in order]))
    omega_pieces[1:] = [held[order.index(k)] for k in range(1, chips)]
    kept, given = call(
        share_body,
        [((skel_rank, middle), F32), ((skel_rank, middle), BF16)],
        partial,
        top_second,
        second[-1],
    )
    got = swapped(given, 1)
    (message,) = call(pair_body, [((skel_rank, middle), BF16)], kept, got)
    messages = [message] + [swapped(message, 2 * k) for k in range(1, chips)]
    (omega,) = call(gather_body, [((skel_rank, middle), BF16)], *omega_pieces)
    (top_omega,) = call(join_body, [((skel_rank, sample_count), F32)], omega, swapped(omega, 1))
    (sample,) = call(
        sample_body,
        [((row_count, sample_count), BF16)],
        own_terms,
        near_first,
        near_second,
        *first,
        *second,
    )
    messages = [messages[k] for k in sorted(range(chips), key=lambda k: (k % 2, k))]
    (total,) = call(total_body, [((skel_rank, middle), BF16)], *messages)
    total, sample, top_omega = lax.optimization_barrier((total, sample, top_omega))
    (top_samples,) = call(join_body, [((skel_rank, sample_count), F32)], total, swapped(total, 1))
    return (sample, top_samples, top_omega)


def solution(mesh):
    placed = (
        P(None, ("blk", "leaf")),
        P(("blk", "leaf"), None),
        P(("blk", "leaf"), None),
        P(("blk", "leaf"), None),
        P(("blk", "leaf"), None),
        P(None, ("blk", "leaf"), None),
        P(None, ("blk", "leaf"), None, None),
    )
    return jax.shard_map(
        on_device,
        mesh=mesh,
        in_specs=placed,
        out_specs=(P(("blk", "leaf"), None), P(("blk", "leaf"), None), P(("blk", "leaf"), None)),
        check_vma=False,
    )
```
